256 devices in a mesh: wide: 16 (over x, z_hi, core), narrow: 16 (over y, z_lo).
Axes of the slice: x: 4, y: 4, z: 8 (z_hi: 2, z_lo: 4; z = z_hi * 4 + z_lo), core: 2. Of those that a mesh axis runs over, the one named last changes fastest.
Arguments:
- images: float32 [16384, 1152], P(('wide', 'narrow')), may hold values from -100 to 100
- texts: float32 [16384, 1152], P(('narrow', 'wide')), may hold values from -100 to 100
- log_scale: float32 [1], replicated, may hold values from 1.6 to 3
- bias: float32 [1], replicated, may hold values from -7 to -4
Outputs:
- loss: float32 [1], replicated
- image_grad: float32 [16384, 1152], P(('wide', 'narrow'))
- text_grad: float32 [16384, 1152], P(('narrow', 'wide'))
The draws below stay inside these ranges and needn't reach their ends.
All inputs are finite; a program needn't handle non-finite values.
Results may differ from the reference program's by a relative error of at most 0.0003.
Values sent between devices are 32-bit elements; how exact they have to be, the bound alone decides.
No kernel may reach another device: no remote copies, remote signals or barrier semaphores. Data moves between devices by JAX's collectives and lax.ppermute only.
A program may use at most 64 MiB of HBM per device.

```python
import jax
import jax.numpy as jnp
from jax import lax

D = 1152
ROWS_DEV = 64
PAIRS = 16384
N_NARROW = 16


def shared_base(key):
    return jnp.clip(jax.random.normal(key, (PAIRS, D), jnp.float32), -5.0, 5.0)


def draw_images(key, part):
    base = shared_base(key)
    key = jax.random.fold_in(key, 11)
    noise = jnp.clip(jax.random.normal(key, (PAIRS, D), jnp.float32), -5.0, 5.0)
    values = base + 0.8 * noise
    return values


def draw_texts(key, part):
    base = shared_base(key)
    key = jax.random.fold_in(key, 23)
    noise = jnp.clip(jax.random.normal(key, (PAIRS, D), jnp.float32), -5.0, 5.0)
    values = base + 0.8 * noise
    return values


def setup_inputs(seed: int = 0) -> dict:
    seeds = jax.random.split(jax.random.key(seed), 5)
    return {
        "images": draw_images(jax.random.fold_in(seeds[4], 71), 0),
        "texts": draw_texts(jax.random.fold_in(seeds[4], 71), 0),
        "log_scale": jnp.clip(jax.random.uniform(seeds[2], (1,), jnp.float32, 1.6, 3.0), 1.6, 3.0),
        "bias": jnp.clip(jax.random.uniform(seeds[3], (1,), jnp.float32, -7.0, -4.0), -7.0, -4.0),
    }


HIGH = lax.Precision.HIGHEST

def unit_rows(values):
    norms = jnp.sqrt(lax.optimization_barrier(jnp.sum(values * values, axis=1, keepdims=True)) + 1e-06)
    return (values / norms, norms)

def reference(images, texts, log_scale, bias):
    scale = jnp.exp(log_scale[0])
    shift = bias[0]
    img_unit, img_norm = unit_rows(images)
    txt_unit, txt_norm = unit_rows(texts)
    block = ROWS_DEV * N_NARROW
    count = PAIRS // block
    columns = jnp.arange(PAIRS, dtype=jnp.int32)

    def one_block(carry, index):
        loss_acc, txt_dir = carry
        start = (index * block).astype(jnp.int32)
        rows_unit = lax.dynamic_slice_in_dim(img_unit, start, block, 0)
        logits = scale * jnp.dot(rows_unit, txt_unit.T, precision=HIGH, preferred_element_type=jnp.float32) + shift
        row_ids = start + jnp.arange(block, dtype=jnp.int32)
        sign = jnp.where(row_ids[:, None] == columns[None, :], 1.0, -1.0).astype(jnp.float32)
        loss_acc = loss_acc + jnp.sum(jax.nn.softplus(-sign * logits))
        coeff = -sign * jax.nn.sigmoid(-sign * logits) * scale
        img_dir = jnp.dot(coeff, txt_unit, precision=HIGH, preferred_element_type=jnp.float32)
        txt_dir = txt_dir + jnp.dot(coeff.T, rows_unit, precision=HIGH, preferred_element_type=jnp.float32)
        return ((loss_acc, txt_dir), img_dir)
    init = (jnp.zeros((), jnp.float32), jnp.zeros((PAIRS, D), jnp.float32))
    (loss_sum, txt_dir), img_dirs = lax.scan(one_block, init, jnp.arange(count, dtype=jnp.int32))
    img_dir = img_dirs.reshape(PAIRS, D)
    image_grad = (img_dir - img_unit * lax.optimization_barrier(jnp.sum(img_dir * img_unit, axis=1, keepdims=True))) / img_norm
    text_grad = (txt_dir - txt_unit * lax.optimization_barrier(jnp.sum(txt_dir * txt_unit, axis=1, keepdims=True))) / txt_norm
    loss = jnp.reshape(loss_sum / PAIRS, (1,))
    return (loss, image_grad, text_grad)
```

```python
import functools

import jax
import jax.numpy as jnp
import numpy as np
from jax import lax
from jax.experimental import pallas as pl
from jax.experimental.pallas import tpu as pltpu
from jax.sharding import PartitionSpec as P

AXES = ("wide", "narrow")
BF = jnp.bfloat16
F32 = jnp.float32
ROWS = 64
BLOCK = 1024
TILE = 256


def flat(x, y, z, c):
    x, y, z, c = x % 4, y % 4, z % 8, c % 2
    return ((x * 2 + z // 4) * 2 + c) * 16 + y * 4 + z % 4


PLACES = [(x, y, z, c) for x in range(4) for y in range(4) for z in range(8) for c in range(2)]


def table(move):
    return [(flat(*p), flat(*move(*p))) for p in PLACES]


def first_of(k, x, y, z, c):
    return (x + k, y, z, c) if c == 0 else (x, y + k, z, c)


def second_of(k, x, y, z, c):
    return (x, y + k, z, c) if c == 0 else (x + k, y, z, c)


def along_of(k, x, y, z, c):
    return (x, y, z + k, c) if c == 0 else (x, y, z - k, c)


def first(k):
    return table(functools.partial(first_of, k))


def second(k):
    return table(functools.partial(second_of, k))


def along(k):
    return table(functools.partial(along_of, k))


def sibling():
    return table(lambda x, y, z, c: (x, y, z, 1 - c))


def send(value, pairs):
    return lax.ppermute(value, AXES, pairs)


def cat(*parts):
    return jnp.concatenate(parts, axis=0)


LINE = (0, -1, 1, 2)
MINE = [(0, 0), (0, 1), (1, 0), (1, 1), (2, 0), (2, 1), (3, 0), (3, 1), (4, 0)]
THEIRS = [(1, 0), (1, 1), (2, 0), (2, 1), (3, 0), (3, 1), (4, 0)]


def shard_tables():
    image = np.zeros((256, 16), np.int32)
    text = np.zeros((256, 16), np.int32)
    for place in PLACES:
        me = flat(*place)
        image[me] = [
            flat(*first_of(k, *second_of(j, *place))) for j in LINE for k in LINE
        ]

        def owner(at, k, sib):
            x, y, z, c = along_of(-k, *at)
            return flat(x, y, z, 1 - c if sib else c)

        x, y, z, c = place
        held = [owner(place, k, sib) for k, sib in MINE]
        held += [owner((x, y, z, 1 - c), k, sib) for k, sib in THEIRS]
        text[me] = [(h % 16) * 16 + h // 16 for h in held]
    return image, text


IMAGE_SHARDS, TEXT_SHARDS = shard_tables()


def gather_images(own):
    fm, fp, f2 = send(own, first(1)), send(own, first(-1)), send(own, first(2))
    line = cat(own, fm, fp, f2)
    lm, lp = send(line, second(1)), send(line, second(-1))
    half = line.shape[0] // 2
    return [line, lm, lp, send(lm[:half], second(1)), send(lp[half:], second(-1))]


def gather_texts(own):
    held = [[own], [send(own, sibling())]]
    for k in range(1, 5):
        for chain in held[: 2 if k < 4 else 1]:
            chain.append(send(chain[-1], along(1)))
    o, b = held
    near = send(cat(o[1], b[1], o[2], b[2]), sibling())
    far = send(cat(o[3], b[3], o[4]), sibling())
    return [o[0], b[0], o[1], b[1], o[2], b[2], o[3], b[3], o[4], near, far]


def reduce_images(parts):
    d0, dm, dp, d2a, d2b = parts
    half = d0.shape[0] // 2
    ra = send(d2a, second(-1))
    rb = send(d2b, second(1))
    tm = send(jnp.concatenate([dm[:half] + ra, dm[half:]], axis=0), second(-1))
    tp = send(jnp.concatenate([dp[:half], dp[half:] + rb], axis=0), second(1))
    line = d0 + tm + tp
    s = line.shape[0] // 4
    em, ep, e2 = line[s : 2 * s], line[2 * s : 3 * s], line[3 * s :]
    return line[:s] + send(em, first(-1)) + send(ep, first(1)) + send(e2, first(2))


def reduce_texts(parts):
    o0, b0, o1, b1, o2, b2, o3, b3, o4, near, far = parts
    s = o0.shape[0]
    back = along(-1)
    far = send(far, sibling())
    near = send(near, sibling())
    o3, b3, o4 = o3 + far[:s], b3 + far[s : 2 * s], o4 + far[2 * s :]
    o1, b1, o2, b2 = (v + near[i * s : (i + 1) * s] for i, v in enumerate((o1, b1, o2, b2)))
    ro = send(o4, back)
    rb = send(b3, back)
    ro = send(o3 + ro, back)
    rb = send(b2 + rb, back)
    ro = send(o2 + ro, back)
    rb = send(b1 + rb, back)
    ro = send(o1 + ro, back)
    return o0 + ro + send(b0 + rb, sibling())


def total_of(value):
    flips = [(0, 0, 0, 1), (1, 0, 0, 0), (2, 0, 0, 0), (0, 1, 0, 0), (0, 2, 0, 0), (0, 0, 1, 0), (0, 0, 2, 0), (0, 0, 4, 0)]
    for flip in flips:
        value = value + send(value, table(lambda *at: [a ^ b for a, b in zip(at, flip)]))
    return value


def split(value):
    hi = value.astype(BF)
    return hi, (value - hi.astype(F32)).astype(BF)


def dot3(a_hi, a_lo, b_hi, b_lo, dims):
    def one(a, b):
        return lax.dot_general(a, b, (dims, ((), ())), preferred_element_type=F32)

    return one(a_hi, b_hi) + (one(a_hi, b_lo) + one(a_lo, b_hi))


def pair_kernel(n_img, n_txt, *refs):
    shards, params, col_ids = refs[:3]
    imgs = refs[3 : 3 + n_img]
    txts = refs[3 + n_img : 3 + n_img + n_txt]
    refs = refs[3 + n_img + n_txt :]
    outs, (loss, c_hi, c_lo, t_hi, t_lo, i_hi, i_lo, acc) = refs[:n_txt], refs[n_txt:]

    for parts, hi, lo in ((imgs, i_hi, i_lo), (txts, t_hi, t_lo)):
        at = 0
        for part in parts:
            rows = part.shape[0]
            for r in range(0, rows, ROWS):
                h, l = split(part[r : r + ROWS, :])
                hi[at + r : at + r + ROWS, :] = h
                lo[at + r : at + r + ROWS, :] = l
            at += rows

    scale, shift = params[0], params[1]
    acc[...] = jnp.zeros_like(acc)

    @pl.loop(0, BLOCK // TILE)
    def _(i):
        rows = pl.ds(pl.multiple_of(i * TILE, TILE), TILE)
        logits = scale * dot3(i_hi[rows, :], i_lo[rows, :], t_hi[...], t_lo[...], ((1,), (1,))) + shift
        at = lax.broadcasted_iota(jnp.int32, (TILE, 1), 0)
        base = jnp.full((TILE, 1), shards[i * 4 + 3], jnp.int32)
        for k in (2, 1, 0):
            base = jnp.where(at < (k + 1) * ROWS, shards[i * 4 + k], base)
        same = (base * ROWS + at % ROWS) == col_ids[...]
        e = jnp.exp(jnp.where(same, -logits, logits))
        p = 1.0 + e
        r = pl.reciprocal(p, approx=True)
        r = r * (2.0 - p * r)
        sig = e * r * scale
        h, l = split(jnp.where(same, -sig, sig))
        c_hi[rows, :] = h
        c_lo[rows, :] = l
        q = TILE // 4
        ea, eb, ec, ed = (e[k * q : (k + 1) * q, :] for k in range(4))
        u = ea + (eb + ea * eb)
        v = ec + (ed + ec * ed)
        g = jnp.log1p(u + (v + u * v))
        acc[...] += jnp.sum(g.reshape(q // 8, 8, BLOCK), axis=0)

    loss[...] = jnp.full(loss.shape, jnp.sum(acc[...]), F32)

    at = 0
    for out in outs:
        rows = out.shape[0]
        cols = pl.ds(at, rows)
        out[...] = dot3(c_hi[:, cols], c_lo[:, cols], i_hi[...], i_lo[...], ((0,), (0,)))
        at += rows


def image_kernel(c_hi, c_lo, t_hi, t_lo, *outs):
    at = 0
    for out in outs:
        rows = pl.ds(at, out.shape[0])
        out[...] = dot3(c_hi[rows, :], c_lo[rows, :], t_hi[...], t_lo[...], ((1,), (0,)))
        at += out.shape[0]


VMEM = pl.BlockSpec(memory_space=pltpu.VMEM)
SMEM = pl.BlockSpec(memory_space=pltpu.SMEM)


def unit_rows(values):
    norms = jnp.sqrt(jnp.sum(values * values, axis=1, keepdims=True) + 1e-06)
    return (values / norms, norms)


def project_back(direction, unit, norms):
    return (direction - unit * jnp.sum(direction * unit, axis=1, keepdims=True)) / norms


def per_device(images, texts, log_scale, bias):
    width = images.shape[1]
    me = lax.axis_index("wide") * 16 + lax.axis_index("narrow")
    shards = lax.dynamic_index_in_dim(jnp.asarray(IMAGE_SHARDS), me, 0, keepdims=False)
    text_shards = lax.dynamic_index_in_dim(jnp.asarray(TEXT_SHARDS), me, 0, keepdims=False)
    col_ids = (text_shards[:, None] * ROWS + jnp.arange(ROWS, dtype=jnp.int32)).reshape(1, BLOCK)
    params = jnp.concatenate([jnp.exp(log_scale), bias])
    img_unit, img_norm = unit_rows(images)
    txt_unit, txt_norm = unit_rows(texts)
    txts = gather_texts(txt_unit)
    imgs = gather_images(img_unit)

    def f32(rows):
        return jax.ShapeDtypeStruct((rows, width), F32)

    def b16(rows, cols):
        return jax.ShapeDtypeStruct((rows, cols), BF)

    pieces = [t.shape[0] for t in txts]
    out = pl.pallas_call(
        functools.partial(pair_kernel, len(imgs), len(txts)),
        out_shape=[f32(r) for r in pieces]
        + [jax.ShapeDtypeStruct((8, 128), F32)]
        + [b16(BLOCK, BLOCK)] * 2
        + [b16(BLOCK, width)] * 2,
        in_specs=[SMEM, SMEM] + [VMEM] * (1 + len(imgs) + len(txts)),
        out_specs=[VMEM] * (len(txts) + 5),
        scratch_shapes=[pltpu.VMEM((BLOCK, width), BF)] * 2 + [pltpu.VMEM((8, BLOCK), F32)],
        compiler_params=pltpu.CompilerParams(vmem_limit_bytes=48 << 20),
        cost_estimate=pl.CostEstimate(flops=14_500_000_000, bytes_accessed=30 << 20, transcendentals=BLOCK * BLOCK * 3),
        name="pairs",
    )(shards, params, col_ids, *imgs, *txts)
    txt_parts, (loss_part, c_hi, c_lo, t_hi, t_lo) = out[: len(txts)], out[len(txts) :]
    img_parts = pl.pallas_call(
        image_kernel,
        out_shape=[f32(t.shape[0]) for t in imgs],
        in_specs=[VMEM] * 4,
        out_specs=[VMEM] * len(imgs),
        compiler_params=pltpu.CompilerParams(vmem_limit_bytes=32 << 20),
        cost_estimate=pl.CostEstimate(flops=7_250_000_000, bytes_accessed=14 << 20, transcendentals=0),
        name="image_dirs",
    )(c_hi, c_lo, t_hi, t_lo)
    txt_own = reduce_texts(txt_parts)
    img_own = reduce_images(img_parts)
    total = total_of(loss_part)[0, 0]
    loss = jnp.reshape(total / 16384.0, (1,))
    image_grad = project_back(img_own, img_unit, img_norm)
    text_grad = project_back(txt_own, txt_unit, txt_norm)
    return (loss, image_grad, text_grad)


def solution(mesh):
    return jax.shard_map(
        per_device,
        mesh=mesh,
        in_specs=(P(("wide", "narrow"), None), P(("narrow", "wide"), None), P(), P()),
        out_specs=(P(), P(("wide", "narrow"), None), P(("narrow", "wide"), None)),
        check_vma=False,
    )
```

```python
import functools

import jax
import jax.numpy as jnp
import numpy as np
from jax import lax
from jax.experimental import pallas as pl
from jax.experimental.pallas import tpu as pltpu
from jax.sharding import PartitionSpec as P

AXES = ("wide", "narrow")
BF = jnp.bfloat16
F32 = jnp.float32
ROWS = 64
BLOCK = 1024
TILE = 256
STEP = 32


def flat(x, y, z, c):
    x, y, z, c = x % 4, y % 4, z % 8, c % 2
    return ((x * 2 + z // 4) * 2 + c) * 16 + y * 4 + z % 4


PLACES = [(x, y, z, c) for x in range(4) for y in range(4) for z in range(8) for c in range(2)]


def table(move):
    return [(flat(*p), flat(*move(*p))) for p in PLACES]


def first_of(k, x, y, z, c):
    return (x + k, y, z, c) if c == 0 else (x, y + k, z, c)


def second_of(k, x, y, z, c):
    return (x, y + k, z, c) if c == 0 else (x + k, y, z, c)


def along_of(k, x, y, z, c):
    return (x, y, z + k, c) if c == 0 else (x, y, z - k, c)


def first(k):
    return table(functools.partial(first_of, k))


def second(k):
    return table(functools.partial(second_of, k))


def along(k):
    return table(functools.partial(along_of, k))


def sibling():
    return table(lambda x, y, z, c: (x, y, z, 1 - c))


def send(value, pairs):
    return lax.ppermute(value, AXES, pairs)


def cat(*parts):
    return jnp.concatenate(parts, axis=0)


LINE = (0, -1, 1, 2)
CHAIN_0 = [(0, 0), (0, 1), (1, 0), (1, 1), (2, 0)]
CHAIN_1 = [(1, 0), (1, 1), (2, 0)]
CHAIN_2 = [(2, 1), (3, 0)]
CHAIN_3 = [(3, 1), (4, 0)]
GROUPS = (8 * ROWS, 4 * ROWS, 4 * ROWS)


def shard_tables():
    image = np.zeros((256, 17), np.int32)
    text = np.zeros((256, 16), np.int32)
    for place in PLACES:
        me = flat(*place)
        x, y, z, c = place
        image[me] = [flat(*first_of(k, *second_of(j, *place))) for j in LINE for k in LINE] + [x * 4 + y]

        def owner(at, k, sib):
            x, y, z, c = along_of(-k, *at)
            return flat(x, y, z, 1 - c if sib else c)

        twin = (x, y, z, 1 - c)
        held = [owner(place, k, sib) for k, sib in CHAIN_0] + [owner(twin, k, sib) for k, sib in CHAIN_1]
        for chain in (CHAIN_2, CHAIN_3):
            held += [owner(at, k, sib) for at in (place, twin) for k, sib in chain]
        text[me] = [(h % 16) * 16 + h // 16 for h in held]
    return image, text


IMAGE_SHARDS, TEXT_SHARDS = shard_tables()


FLIPS = [(0, 0, 4, 0), (0, 0, 2, 0), (0, 0, 1, 0), (0, 0, 0, 1)]


def flip_of(k, *at):
    return [a ^ b for a, b in zip(at, FLIPS[k])]


def flipped(value, k):
    return send(value, table(functools.partial(flip_of, k)))


def split(value):
    hi = value.astype(BF)
    return hi, (value - hi.astype(F32)).astype(BF)


def dot3(a_hi, a_lo, b_hi, b_lo, dims):
    def one(a, b):
        return lax.dot_general(a, b, (dims, ((), ())), preferred_element_type=F32)

    return one(a_hi, b_hi) + (one(a_hi, b_lo) + one(a_lo, b_hi))


def split_into(hi, lo, parts, spans):
    at = 0
    for p, start, count in spans:

        @pl.loop(0, count // 16)
        def _(i, part=parts[p], start=start, at=at):
            h, l = split(part[pl.ds(pl.multiple_of(start + i * 16, 16), 16), :])
            rows = pl.ds(pl.multiple_of(at + i * 16, 16), 16)
            hi[rows, :] = h
            lo[rows, :] = l

        at += count


def split_kernel(spans, *refs):
    split_into(refs[-2], refs[-1], refs[:-2], spans)


def coefficients(first_shard, shards, params, col_ids, logits, stores):
    scale, shift = params[0], params[1]
    at = lax.broadcasted_iota(jnp.int32, (STEP, 1), 0)
    cols = logits.shape[1]
    acc = jnp.zeros((8, 128), F32)
    for k, (c_hi, c_lo) in enumerate(stores):

        def body(i, acc, k=k, c_hi=c_hi, c_lo=c_lo):
            rows = pl.ds(pl.multiple_of(i * STEP, STEP), STEP)
            source = pl.ds(pl.multiple_of(k * TILE + i * STEP, STEP), STEP)
            shard = shards[first_shard + k * 4 + i // (ROWS // STEP)]
            row_ids = shard * ROWS + (i % (ROWS // STEP)) * STEP + at
            for c in range(0, cols, 128):
                here = slice(c, c + 128)
                x = scale * logits[source, here] + shift
                same = row_ids == col_ids[:, here]
                e = jnp.exp(jnp.where(same, -x, x))
                p = 1.0 + e
                r = pl.reciprocal(p, approx=True)
                r = r * (2.0 - p * r)
                sig = e * r * scale
                h, l = split(jnp.where(same, -sig, sig))
                c_hi[rows, here] = h
                c_lo[rows, here] = l
                q = STEP // 4
                ea, eb, ec, ed = (e[j * q : (j + 1) * q, :] for j in range(4))
                u = ea + (eb + ea * eb)
                v = ec + (ed + ec * ed)
                acc = acc + jnp.log1p(u + (v + u * v))
            return acc

        acc = lax.fori_loop(0, TILE // STEP, body, acc)
    return acc


def near_kernel(k, spans, shards, params, col_ids, t_hi, t_lo, *refs):
    parts, (c_hi, c_lo, i_hi, i_lo, loss, logits) = refs[:-6], refs[-6:]
    split_into(i_hi, i_lo, parts, spans)
    logits[...] = dot3(i_hi[...], i_lo[...], t_hi[...], t_lo[...], ((1,), (1,)))
    loss[...] = coefficients(k * 4, shards, params, col_ids, logits, [(c_hi, c_lo)])


def group_kernel(count, final, shards, params, col_ids, *refs):
    lines, parts, losses = refs[:8], refs[8:10], refs[10 : 10 + count]
    stores, (t_hi, t_lo, loss, logits) = refs[10 + count : 18 + count], refs[18 + count :]
    split_into(t_hi, t_lo, parts, [(0, 0, parts[0].shape[0]), (1, 0, parts[1].shape[0])])
    for k in range(4):
        logits[k * TILE : (k + 1) * TILE, :] = dot3(
            lines[2 * k][...], lines[2 * k + 1][...], t_hi[...], t_lo[...], ((1,), (1,))
        )
    pairs = [(stores[2 * k], stores[2 * k + 1]) for k in range(4)]
    acc = coefficients(0, shards, params, col_ids, logits, pairs)
    for part in losses:
        acc = acc + part[...]
    loss[...] = jnp.full(loss.shape, jnp.sum(acc), F32) if final else acc


def fold_kernel(shards, loss, flip, am, bm, ap, bp, down, up, to_m, to_p, mine):
    s = ROWS
    total = (loss[...] + flip[...])[:1, :1]
    row = lax.broadcasted_iota(jnp.int32, mine.shape, 0)
    lane = lax.broadcasted_iota(jnp.int32, mine.shape, 1)
    value = jnp.where((row == 0) & (lane == shards[16]), total, 0.0)
    mine[...] = value
    to_m[:s, :] = am[:s, :] + down[:s, :]
    to_m[s : 2 * s, :] = am[s:, :]
    to_m[2 * s : 3 * s, :] = bm[:s, :] + down[s:, :]
    to_m[3 * s : 4 * s, :] = bm[s:, :]
    to_m[4 * s :, :] = value
    to_p[:s, :] = ap[:s, :]
    to_p[s : 2 * s, :] = ap[s:, :] + up[:s, :]
    to_p[2 * s : 3 * s, :] = bp[:s, :]
    to_p[3 * s : 4 * s, :] = bp[s:, :] + up[s:, :]
    to_p[4 * s :, :] = value


def gate_kernel(count, rule, *refs):
    ins, outs = refs[:count], refs[count:]
    for out, pieces in zip(outs, rule):
        at = 0
        for rows, terms in pieces:
            total = None
            for p, start in terms:
                v = ins[p][start : start + rows, :]
                total = v if total is None else total + v
            out[at : at + rows, :] = total
            at += rows


def store(outs, rule, value):
    for out, spans in zip(outs, rule):
        at = 0
        for start, rows in spans:
            out[at : at + rows, :] = value[start : start + rows, :]
            at += rows


def image_kernel(rule, *refs):
    ins, outs = refs[:12], refs[12:]
    total = None
    for g in range(3):
        d = dot3(*(r[...] for r in ins[4 * g : 4 * g + 4]), ((1,), (0,)))
        total = d if total is None else total + d
    store(outs, rule, total)


def text_kernel(rule, *refs):
    ins, outs = refs[:16], refs[16:]
    total = None
    for k in range(4):
        d = dot3(*(r[...] for r in ins[2 * k : 2 * k + 2] + ins[8 + 2 * k : 10 + 2 * k]), ((0,), (0,)))
        total = d if total is None else total + d
    store(outs, rule, total)


VMEM = pl.BlockSpec(memory_space=pltpu.VMEM)
SMEM = pl.BlockSpec(memory_space=pltpu.SMEM)


def unit_kernel(images, texts, iu, tu, x, y, sems):
    copies = [pltpu.make_async_copy(a, b, sems.at[i]) for i, (a, b) in enumerate(((images, x), (texts, y)))]
    for copy in copies:
        copy.start()
    for copy, source, out in zip(copies, (x, y), (iu, tu)):
        copy.wait()
        v = source[...]
        out[...] = v / jnp.sqrt(jnp.sum(v * v, axis=1, keepdims=True) + 1e-06)


def project(parts, source, out):
    d = parts[0]
    for part in parts[1:]:
        d = d + part
    x = source[...]
    norm = jnp.sqrt(jnp.sum(x * x, axis=1, keepdims=True) + 1e-06)
    u = x / norm
    out[...] = (d - u * jnp.sum(d * u, axis=1, keepdims=True)) / norm


def last_kernel(own, em, ep, e2, o0, zo, sb, images, texts, loss, image_grad, text_grad, x, y, sems):
    s = ROWS
    copies = [pltpu.make_async_copy(a, b, sems.at[i]) for i, (a, b) in enumerate(((images, x), (texts, y)))]
    for copy in copies:
        copy.start()
    for copy in copies:
        copy.wait()
    project([own[:s, :], em[:s, :], ep[:s, :], e2[:s, :]], x, image_grad)
    project([o0[...], zo[...], sb[...]], y, text_grad)
    rows = own[s:, :] + em[s:, :] + ep[s:, :] + e2[s:, :]
    loss[0] = jnp.sum(rows) / 16384.0


def shape(rows, cols, dtype=F32):
    return jax.ShapeDtypeStruct((rows, cols), dtype)


class Chain:
    def __init__(self):
        self.token = None

    def call(self, kernel, name, outs, ins, deps=(), scratch=(), vmem=16, special=0, out_specs=None, raw=0, us=0.1):
        outs, ins, deps = tuple(outs), list(ins), list(deps)
        if self.token is not None and not any(self.token is v for v in ins + deps):
            deps.append(self.token)
        count = len(ins)
        anywhere = pl.BlockSpec(memory_space=pl.ANY)

        def body(*refs):
            kernel(*refs[:count], *refs[count + len(deps) :])

        out = pl.pallas_call(
            body,
            out_shape=outs,
            in_specs=[SMEM] * special + [VMEM] * (count - special - raw) + [anywhere] * (raw + len(deps)),
            out_specs=out_specs or (VMEM,) * len(outs),
            scratch_shapes=scratch,
            compiler_params=pltpu.CompilerParams(vmem_limit_bytes=vmem << 20),
            cost_estimate=pl.CostEstimate(flops=int(us * 1e9), bytes_accessed=1 << 16, transcendentals=0),
            name=name,
        )(*ins, *deps)
        self.token = out[-1]
        return out

    def gate(self, name, rule, deps=()):
        ins = []

        def place(array):
            for i, known in enumerate(ins):
                if known is array:
                    return i
            ins.append(array)
            return len(ins) - 1

        rule = [[(rows, [(place(v), start) for v, start in terms]) for rows, terms in pieces] for pieces in rule]
        outs = [shape(sum(rows for rows, _ in pieces), ins[pieces[0][1][0][0]].shape[1]) for pieces in rule]
        return self.call(functools.partial(gate_kernel, len(ins), rule), name, outs, ins, deps)


def per_device(images, texts, log_scale, bias):
    width = images.shape[1]
    s = ROWS
    me = lax.axis_index("wide") * 16 + lax.axis_index("narrow")
    shards = lax.dynamic_index_in_dim(jnp.asarray(IMAGE_SHARDS), me, 0, keepdims=False)
    text_shards = lax.dynamic_index_in_dim(jnp.asarray(TEXT_SHARDS), me, 0, keepdims=False)
    col_ids = (text_shards[:, None] * ROWS + jnp.arange(ROWS, dtype=jnp.int32)).reshape(1, BLOCK)
    params = jnp.concatenate([jnp.exp(log_scale), bias])
    ids = [col_ids[:, : 8 * s], col_ids[:, 8 * s : 12 * s], col_ids[:, 12 * s :]]
    swap, ahead, back = sibling(), along(1), along(-1)
    up, down = second(1), second(-1)
    chain = Chain()
    call, gate = chain.call, chain.gate

    def copy(rows, *pieces):
        return [(r, [(v, start)]) for r, (v, start) in zip(rows, pieces)]

    buffers = [pltpu.VMEM((s, width), F32)] * 2 + [pltpu.SemaphoreType.DMA((2,))]
    iu, tu = call(unit_kernel, "units", [shape(s, width)] * 2, [images, texts], scratch=buffers, raw=2)
    fm, fp, f2 = send(iu, first(1)), send(iu, first(-1)), send(iu, first(2))
    o1, b0 = send(tu, ahead), send(tu, swap)
    (zb,) = gate("gate_z1", [copy((s, s), (b0, 0), (o1, 0))])
    z2 = send(zb, ahead)
    (l0,) = gate("gate_l", [copy((s, s, s, s), (iu, 0), (fm, 0), (fp, 0), (f2, 0))])
    lm, lp = send(l0, up), send(l0, down)
    zz2, sw1 = gate("gate_z2", [copy((2 * s,), (z2, 0)), copy((s, 2 * s), (o1, 0), (z2, 0))], [shards, params, *ids])
    z3, s1 = send(zz2, ahead), send(sw1, swap)
    near = call(
        functools.partial(split_kernel, [(0, 0, s), (1, 0, s), (2, 0, s), (3, 0, 2 * s), (4, 0, 3 * s)]),
        "split_near",
        [shape(8 * s, width, BF)] * 2,
        [tu, b0, o1, zz2, s1],
    )

    def near_pairs(k, parts, spans):
        return call(
            functools.partial(near_kernel, k, spans),
            f"near{k}",
            [shape(TILE, GROUPS[0], BF)] * 2 + [shape(TILE, width, BF)] * 2 + [shape(8, 128)],
            [shards, params, ids[0], *near, *parts],
            scratch=[pltpu.VMEM((TILE, GROUPS[0]), F32)],
            special=2,
            us=2.5,
        )

    one = [(0, 0, 4 * s)]
    n0 = near_pairs(0, [l0], one)
    (zz3,) = gate("gate_z3", [copy((2 * s,), (z3, 0))])
    z4, s2 = send(zz3, ahead), send(zz3, swap)
    cu, cd = gate("gate_c", [copy((s, s), (lm, 0), (lm, 2 * s)), copy((s, s), (lp, s), (lp, 3 * s))])
    cu, cd = send(cu, up), send(cd, down)
    n1 = near_pairs(1, [lm], one)
    n2 = near_pairs(2, [lp], one)
    (zz4,) = gate("gate_z4", [copy((2 * s,), (z4, 0))])
    s3 = send(zz4, swap)
    n3 = near_pairs(3, [cu, cd], [(0, 0, s), (1, 0, s), (0, s, s), (1, s, s)])
    n = [n0, n1, n2, n3]
    lines = [v for k in range(4) for v in n[k][2:4]]

    def group_pairs(g, name, parts, losses):
        out = call(
            functools.partial(group_kernel, len(losses), g == 2),
            name,
            [shape(TILE, GROUPS[g], BF)] * 8 + [shape(GROUPS[g], width, BF)] * 2 + [shape(8, 128)],
            [shards, params, ids[g], *lines, *parts, *losses],
            scratch=[pltpu.VMEM((BLOCK, GROUPS[g]), F32)],
            special=2,
            us=4.5,
        )
        return out[:8], out[8:10], out[10]

    mid_coeffs, mid, loss = group_pairs(1, "mid", [zz3, s2], [n[k][4] for k in range(4)])
    far_coeffs, far, loss = group_pairs(2, "far", [zz4, s3], [loss])
    near_coeffs = [v for k in range(4) for v in n[k][:2]]

    def text_dirs(name, coeffs, rule):
        outs = [shape(sum(r for _, r in spans), width) for spans in rule]
        return call(functools.partial(text_kernel, rule), name, outs, [*coeffs, *lines], us=coeffs[0].shape[1] / 116)

    def image_dirs(k, rule):
        outs = [shape(sum(r for _, r in spans), width) for spans in rule]
        ins = [*near_coeffs[2 * k : 2 * k + 2], *near, *mid_coeffs[2 * k : 2 * k + 2], *mid]
        ins += [*far_coeffs[2 * k : 2 * k + 2], *far]
        return call(functools.partial(image_kernel, rule), f"image{k}", outs, ins, us=2.2)

    def add_loss(name, loss, flip):
        return gate(name, [[(8, [(loss, 0), (flip, 0)])]])[0]

    def add_loss(name, loss, flip):
        return gate(name, [[(8, [(loss, 0), (flip, 0)])]])[0]

    f = flipped(loss, 0)
    halves = [[(0, 2 * s)], [(2 * s, 2 * s)]]
    p34, sw = text_dirs("text_far", far_coeffs, halves)
    s34 = send(sw, swap)
    c_dn, c_up = image_dirs(3, [[(0, s), (2 * s, s)], [(s, s), (3 * s, s)]])
    c_dn, c_up = send(c_dn, down), send(c_up, up)
    (z_out,) = gate("gate_q1", [[(2 * s, [(p34, 0), (s34, 0)])]])
    zq = send(z_out, back)
    loss = add_loss("loss1", loss, f)
    f = flipped(loss, 1)
    p23, sw = text_dirs("text_mid", mid_coeffs, halves)
    s23 = send(sw, swap)
    im1, ib1 = image_dirs(1, halves)
    loss = add_loss("loss2", loss, f)
    f = flipped(loss, 2)
    t_o0, t_b0, t_o1, t_12, sw = text_dirs(
        "text_near",
        near_coeffs,
        [[(0, s)], [(s, s)], [(2 * s, s)], [(3 * s, 2 * s)], [(5 * s, 3 * s)]],
    )
    s12 = send(sw, swap)
    (z_out,) = gate("gate_q2", [[(2 * s, [(p23, 0), (s23, 0), (zq, 0)])]])
    zq = send(z_out, back)
    im2, ib2 = image_dirs(2, halves)
    loss = add_loss("loss3", loss, f)
    f = flipped(loss, 3)
    im0, ib0 = image_dirs(0, halves)
    (z_out,) = gate("gate_q3", [[(2 * s, [(t_12, 0), (s12, s), (zq, 0)])]])
    zq = send(z_out, back)
    to_m, to_p, mine = call(
        fold_kernel,
        "fold",
        [shape(4 * s + 8, width)] * 2 + [shape(8, width)],
        [shards, loss, f, im1, ib1, im2, ib2, c_dn, c_up],
        special=1,
    )
    lm, lp, across = send(to_m, down), send(to_p, up), send(mine, second(2))
    rows = (8, [(mine, 0), (lm, 4 * s), (lp, 4 * s), (across, 0)])
    own, e_fm, e_fp, e_f2 = gate(
        "gate_q4",
        [
            [(s, [(im0, 0), (lm, 0), (lp, 0)]), rows],
            [(s, [(im0, s), (lm, s), (lp, s)]), rows],
            [(s, [(ib0, 0), (lm, 2 * s), (lp, 2 * s)]), rows],
            [(s, [(ib0, s), (lm, 3 * s), (lp, 3 * s)]), rows],
        ],
    )
    em, ep, e2 = send(e_fm, first(-1)), send(e_fp, first(1)), send(e_f2, first(2))
    o_out, b_out = gate("gate_q5", [[(s, [(t_o1, 0), (s12, 0), (zq, s)])], [(s, [(t_b0, 0), (zq, 0)])]])
    zo, sb = send(o_out, back), send(b_out, swap)
    loss, image_grad, text_grad = call(
        last_kernel,
        "last",
        [jax.ShapeDtypeStruct((1,), F32)] + [shape(s, width)] * 2,
        [own, em, ep, e2, t_o0, zo, sb, images, texts],
        scratch=buffers,
        out_specs=(SMEM, VMEM, VMEM),
        raw=2,
    )
    return (loss, image_grad, text_grad)


def solution(mesh):
    return jax.shard_map(
        per_device,
        mesh=mesh,
        in_specs=(P(("wide", "narrow"), None), P(("narrow", "wide"), None), P(), P()),
        out_specs=(P(), P(("wide", "narrow"), None), P(("narrow", "wide"), None)),
        check_vma=False,
    )
```

```python
import functools

import jax
import jax.numpy as jnp
import numpy as np
from jax import lax
from jax.experimental import pallas as pl
from jax.experimental.pallas import tpu as pltpu
from jax.sharding import PartitionSpec as P

AXES = ("wide", "narrow")
BF = jnp.bfloat16
F32 = jnp.float32
ROWS = 64
BLOCK = 1024
TILE = 256
STEP = 32


def flat(x, y, z, c):
    x, y, z, c = x % 4, y % 4, z % 8, c % 2
    return ((x * 2 + z // 4) * 2 + c) * 16 + y * 4 + z % 4


PLACES = [(x, y, z, c) for x in range(4) for y in range(4) for z in range(8) for c in range(2)]


def table(move):
    return [(flat(*p), flat(*move(*p))) for p in PLACES]


def first_of(k, x, y, z, c):
    return (x + k, y, z, c) if c == 0 else (x, y + k, z, c)


def second_of(k, x, y, z, c):
    return (x, y + k, z, c) if c == 0 else (x + k, y, z, c)


def along_of(k, x, y, z, c):
    return (x, y, z + k, c) if c == 0 else (x, y, z - k, c)


def first(k):
    return table(functools.partial(first_of, k))


def second(k):
    return table(functools.partial(second_of, k))


def along(k):
    return table(functools.partial(along_of, k))


def sibling():
    return table(lambda x, y, z, c: (x, y, z, 1 - c))


def send(value, pairs):
    return lax.ppermute(value, AXES, pairs)


def cat(*parts):
    return jnp.concatenate(parts, axis=0)


LINE = (0, -1, 1, 2)
CHAIN_0 = [(0, 0), (0, 1), (1, 0), (1, 1), (2, 0)]
CHAIN_1 = [(1, 0), (1, 1), (2, 0)]
CHAIN_2 = [(2, 1), (3, 0)]
CHAIN_3 = [(3, 1), (4, 0)]
U = (2.2, 2.2, 8, 8, 1, 8, 4, 4)
GROUPS = (8 * ROWS, 4 * ROWS, 4 * ROWS)


def shard_tables():
    image = np.zeros((256, 17), np.int32)
    text = np.zeros((256, 16), np.int32)
    for place in PLACES:
        me = flat(*place)
        x, y, z, c = place
        image[me] = [flat(*first_of(k, *second_of(j, *place))) for j in LINE for k in LINE] + [x * 4 + y]

        def owner(at, k, sib):
            x, y, z, c = along_of(-k, *at)
            return flat(x, y, z, 1 - c if sib else c)

        twin = (x, y, z, 1 - c)
        held = [owner(place, k, sib) for k, sib in CHAIN_0] + [owner(twin, k, sib) for k, sib in CHAIN_1]
        for chain in (CHAIN_2, CHAIN_3):
            held += [owner(at, k, sib) for at in (place, twin) for k, sib in chain]
        text[me] = [(h % 16) * 16 + h // 16 for h in held]
    return image, text


IMAGE_SHARDS, TEXT_SHARDS = shard_tables()


FLIPS = [(0, 0, 4, 0), (0, 0, 2, 0), (0, 0, 1, 0), (0, 0, 0, 1)]


def flip_of(k, *at):
    return [a ^ b for a, b in zip(at, FLIPS[k])]


def flipped(value, k):
    return send(value, table(functools.partial(flip_of, k)))


def split(value):
    hi = value.astype(BF)
    return hi, (value - hi.astype(F32)).astype(BF)


def dot3(a_hi, a_lo, b_hi, b_lo, dims):
    def one(a, b):
        return lax.dot_general(a, b, (dims, ((), ())), preferred_element_type=F32)

    return one(a_hi, b_hi) + (one(a_hi, b_lo) + one(a_lo, b_hi))


def split_into(hi, lo, parts, spans):
    at = 0
    for p, start, count in spans:

        @pl.loop(0, count // 16)
        def _(i, part=parts[p], start=start, at=at):
            h, l = split(part[pl.ds(pl.multiple_of(start + i * 16, 16), 16), :])
            rows = pl.ds(pl.multiple_of(at + i * 16, 16), 16)
            hi[rows, :] = h
            lo[rows, :] = l

        at += count


def split_kernel(spans, *refs):
    split_into(refs[-2], refs[-1], refs[:-2], spans)


def coefficients(first_shard, shards, params, col_ids, logits, stores):
    scale, shift = params[0], params[1]
    at = lax.broadcasted_iota(jnp.int32, (STEP, 1), 0)
    cols = logits.shape[1]
    acc = jnp.zeros((8, 128), F32)
    for k, (c_hi, c_lo) in enumerate(stores):

        def body(i, acc, k=k, c_hi=c_hi, c_lo=c_lo):
            rows = pl.ds(pl.multiple_of(i * STEP, STEP), STEP)
            source = pl.ds(pl.multiple_of(k * TILE + i * STEP, STEP), STEP)
            shard = shards[first_shard + k * 4 + i // (ROWS // STEP)]
            row_ids = shard * ROWS + (i % (ROWS // STEP)) * STEP + at
            for c in range(0, cols, 128):
                here = slice(c, c + 128)
                x = scale * logits[source, here] + shift
                same = row_ids == col_ids[:, here]
                e = jnp.exp(jnp.where(same, -x, x))
                p = 1.0 + e
                r = pl.reciprocal(p, approx=True)
                r = r * (2.0 - p * r)
                sig = e * r * scale
                h, l = split(jnp.where(same, -sig, sig))
                c_hi[rows, here] = h
                c_lo[rows, here] = l
                q = STEP // 4
                ea, eb, ec, ed = (e[j * q : (j + 1) * q, :] for j in range(4))
                u = ea + (eb + ea * eb)
                v = ec + (ed + ec * ed)
                acc = acc + jnp.log1p(u + (v + u * v))
            return acc

        acc = lax.fori_loop(0, TILE // STEP, body, acc)
    return acc


def near_kernel(k, spans, shards, params, col_ids, t_hi, t_lo, *refs):
    parts, (c_hi, c_lo, i_hi, i_lo, loss, logits) = refs[:-6], refs[-6:]
    split_into(i_hi, i_lo, parts, spans)
    logits[...] = dot3(i_hi[...], i_lo[...], t_hi[...], t_lo[...], ((1,), (1,)))
    loss[...] = coefficients(k * 4, shards, params, col_ids, logits, [(c_hi, c_lo)])


def group_kernel(count, final, shards, params, col_ids, *refs):
    lines, parts, losses = refs[:8], refs[8:10], refs[10 : 10 + count]
    stores, (t_hi, t_lo, loss, logits) = refs[10 + count : 18 + count], refs[18 + count :]
    split_into(t_hi, t_lo, parts, [(0, 0, parts[0].shape[0]), (1, 0, parts[1].shape[0])])
    for k in range(4):
        logits[k * TILE : (k + 1) * TILE, :] = dot3(
            lines[2 * k][...], lines[2 * k + 1][...], t_hi[...], t_lo[...], ((1,), (1,))
        )
    pairs = [(stores[2 * k], stores[2 * k + 1]) for k in range(4)]
    acc = coefficients(0, shards, params, col_ids, logits, pairs)
    for part in losses:
        acc = acc + part[...]
    loss[...] = jnp.full(loss.shape, jnp.sum(acc), F32) if final else acc


def fold_kernel(shards, loss, flip, am, bm, ap, bp, down, up, to_m, to_p, mine):
    s = ROWS
    total = (loss[...] + flip[...])[:1, :1]
    row = lax.broadcasted_iota(jnp.int32, mine.shape, 0)
    lane = lax.broadcasted_iota(jnp.int32, mine.shape, 1)
    value = jnp.where((row == 0) & (lane == shards[16]), total, 0.0)
    mine[...] = value
    to_m[:s, :] = am[:s, :] + down[:s, :]
    to_m[s : 2 * s, :] = am[s:, :]
    to_m[2 * s : 3 * s, :] = bm[:s, :] + down[s:, :]
    to_m[3 * s : 4 * s, :] = bm[s:, :]
    to_m[4 * s :, :] = value
    to_p[:s, :] = ap[:s, :]
    to_p[s : 2 * s, :] = ap[s:, :] + up[:s, :]
    to_p[2 * s : 3 * s, :] = bp[:s, :]
    to_p[3 * s : 4 * s, :] = bp[s:, :] + up[s:, :]
    to_p[4 * s :, :] = value


def gate_kernel(count, rule, *refs):
    ins, outs = refs[:count], refs[count:]
    for out, pieces in zip(outs, rule):
        at = 0
        for rows, terms in pieces:
            total = None
            for p, start in terms:
                v = ins[p][start : start + rows, :]
                total = v if total is None else total + v
            out[at : at + rows, :] = total
            at += rows


def store(outs, rule, value):
    for out, spans in zip(outs, rule):
        at = 0
        for start, rows in spans:
            out[at : at + rows, :] = value[start : start + rows, :]
            at += rows


def image_kernel(rule, *refs):
    ins, outs = refs[:12], refs[12:]
    total = None
    for g in range(3):
        d = dot3(*(r[...] for r in ins[4 * g : 4 * g + 4]), ((1,), (0,)))
        total = d if total is None else total + d
    store(outs, rule, total)


def text_kernel(start, stop, rule, *refs):
    ins, outs = refs[:16], refs[16:]
    total = None
    for k in range(4):
        c_hi, c_lo = (r[:, start:stop] for r in ins[2 * k : 2 * k + 2])
        d = dot3(c_hi, c_lo, ins[8 + 2 * k][...], ins[9 + 2 * k][...], ((0,), (0,)))
        total = d if total is None else total + d
    store(outs, rule, total)


VMEM = pl.BlockSpec(memory_space=pltpu.VMEM)
SMEM = pl.BlockSpec(memory_space=pltpu.SMEM)


def unit_kernel(images, texts, iu, tu, x, y, sems):
    copies = [pltpu.make_async_copy(a, b, sems.at[i]) for i, (a, b) in enumerate(((images, x), (texts, y)))]
    for copy in copies:
        copy.start()
    for copy, source, out in zip(copies, (x, y), (iu, tu)):
        copy.wait()
        v = source[...]
        out[...] = v / jnp.sqrt(jnp.sum(v * v, axis=1, keepdims=True) + 1e-06)


def project(parts, source, out):
    d = parts[0]
    for part in parts[1:]:
        d = d + part
    x = source[...]
    norm = jnp.sqrt(jnp.sum(x * x, axis=1, keepdims=True) + 1e-06)
    u = x / norm
    out[...] = (d - u * jnp.sum(d * u, axis=1, keepdims=True)) / norm


def last_kernel(own, em, ep, e2, o0, zo, sb, images, texts, loss, image_grad, text_grad, x, y, sems):
    s = ROWS
    copies = [pltpu.make_async_copy(a, b, sems.at[i]) for i, (a, b) in enumerate(((images, x), (texts, y)))]
    for copy in copies:
        copy.start()
    for copy in copies:
        copy.wait()
    project([own[:s, :], em[:s, :], ep[:s, :], e2[:s, :]], x, image_grad)
    project([o0[...], zo[...], sb[...]], y, text_grad)
    rows = own[s:, :] + em[s:, :] + ep[s:, :] + e2[s:, :]
    loss[0] = jnp.sum(rows) / 16384.0


def shape(rows, cols, dtype=F32):
    return jax.ShapeDtypeStruct((rows, cols), dtype)


class Chain:
    def __init__(self):
        self.token = None

    def call(self, kernel, name, outs, ins, deps=(), scratch=(), vmem=16, special=0, out_specs=None, raw=0, us=0.1):
        outs, ins, deps = tuple(outs), list(ins), list(deps)
        if self.token is not None and not any(self.token is v for v in ins + deps):
            deps.append(self.token)
        count = len(ins)
        anywhere = pl.BlockSpec(memory_space=pl.ANY)

        def body(*refs):
            kernel(*refs[:count], *refs[count + len(deps) :])

        out = pl.pallas_call(
            body,
            out_shape=outs,
            in_specs=[SMEM] * special + [VMEM] * (count - special - raw) + [pl.BlockSpec(memory_space=pltpu.HBM)] * raw + [anywhere] * len(deps),
            out_specs=out_specs or (VMEM,) * len(outs),
            scratch_shapes=scratch,
            compiler_params=pltpu.CompilerParams(vmem_limit_bytes=vmem << 20),
            cost_estimate=pl.CostEstimate(flops=int(us * 1e9), bytes_accessed=1 << 16, transcendentals=0),
            name=name,
        )(*ins, *deps)
        self.token = out[-1]
        return out

    def gate(self, name, rule, deps=()):
        ins = []

        def place(array):
            for i, known in enumerate(ins):
                if known is array:
                    return i
            ins.append(array)
            return len(ins) - 1

        rule = [[(rows, [(place(v), start) for v, start in terms]) for rows, terms in pieces] for pieces in rule]
        outs = [shape(sum(rows for rows, _ in pieces), ins[pieces[0][1][0][0]].shape[1]) for pieces in rule]
        return self.call(functools.partial(gate_kernel, len(ins), rule), name, outs, ins, deps)


def per_device(images, texts, log_scale, bias):
    width = images.shape[1]
    s = ROWS
    me = lax.axis_index("wide") * 16 + lax.axis_index("narrow")
    shards = lax.dynamic_index_in_dim(jnp.asarray(IMAGE_SHARDS), me, 0, keepdims=False)
    text_shards = lax.dynamic_index_in_dim(jnp.asarray(TEXT_SHARDS), me, 0, keepdims=False)
    col_ids = (text_shards[:, None] * ROWS + jnp.arange(ROWS, dtype=jnp.int32)).reshape(1, BLOCK)
    params = jnp.concatenate([jnp.exp(log_scale), bias])
    ids = [col_ids[:, : 8 * s], col_ids[:, 8 * s : 12 * s], col_ids[:, 12 * s :]]
    swap, ahead, back = sibling(), along(1), along(-1)
    up, down = second(1), second(-1)
    chain = Chain()
    call, gate = chain.call, chain.gate

    def copy(rows, *pieces):
        return [(r, [(v, start)]) for r, (v, start) in zip(rows, pieces)]

    buffers = [pltpu.VMEM((s, width), F32)] * 2 + [pltpu.SemaphoreType.DMA((2,))]
    iu, tu = call(unit_kernel, "units", [shape(s, width)] * 2, [images, texts], scratch=buffers, raw=2)
    fm, fp, f2 = send(iu, first(1)), send(iu, first(-1)), send(iu, first(2))
    o1, b0 = send(tu, ahead), send(tu, swap)
    (zb,) = gate("gate_z1", [copy((s, s), (b0, 0), (o1, 0))])
    z2 = send(zb, ahead)
    (l0,) = gate("gate_l", [copy((s, s, s, s), (iu, 0), (fm, 0), (fp, 0), (f2, 0))])
    lm, lp = send(l0, up), send(l0, down)
    zz2, sw1 = gate("gate_z2", [copy((2 * s,), (z2, 0)), copy((s, 2 * s), (o1, 0), (z2, 0))], [shards, params, *ids])
    z3, s1 = send(zz2, ahead), send(sw1, swap)
    near = call(
        functools.partial(split_kernel, [(0, 0, s), (1, 0, s), (2, 0, s), (3, 0, 2 * s), (4, 0, 3 * s)]),
        "split_near",
        [shape(8 * s, width, BF)] * 2,
        [tu, b0, o1, zz2, s1],
    )

    def near_pairs(k, parts, spans):
        return call(
            functools.partial(near_kernel, k, spans),
            f"near{k}",
            [shape(TILE, GROUPS[0], BF)] * 2 + [shape(TILE, width, BF)] * 2 + [shape(8, 128)],
            [shards, params, ids[0], *near, *parts],
            scratch=[pltpu.VMEM((TILE, GROUPS[0]), F32)],
            special=2,
            us=2.5,
        )

    one = [(0, 0, 4 * s)]
    n0 = near_pairs(0, [l0], one)
    (zz3,) = gate("gate_z3", [copy((2 * s,), (z3, 0))])
    z4, s2 = send(zz3, ahead), send(zz3, swap)
    cu, cd = gate("gate_c", [copy((s, s), (lm, 0), (lm, 2 * s)), copy((s, s), (lp, s), (lp, 3 * s))])
    cu, cd = send(cu, up), send(cd, down)
    n1 = near_pairs(1, [lm], one)
    n2 = near_pairs(2, [lp], one)
    (zz4,) = gate("gate_z4", [copy((2 * s,), (z4, 0))])
    s3 = send(zz4, swap)
    n3 = near_pairs(3, [cu, cd], [(0, 0, s), (1, 0, s), (0, s, s), (1, s, s)])
    n = [n0, n1, n2, n3]
    lines = [v for k in range(4) for v in n[k][2:4]]

    def group_pairs(g, name, parts, losses):
        out = call(
            functools.partial(group_kernel, len(losses), g == 2),
            name,
            [shape(TILE, GROUPS[g], BF)] * 8 + [shape(GROUPS[g], width, BF)] * 2 + [shape(8, 128)],
            [shards, params, ids[g], *lines, *parts, *losses],
            scratch=[pltpu.VMEM((BLOCK, GROUPS[g]), F32)],
            special=2,
            us=4.5,
        )
        return out[:8], out[8:10], out[10]

    mid_coeffs, mid, loss = group_pairs(1, "mid", [zz3, s2], [n[k][4] for k in range(4)])
    far_coeffs, far, loss = group_pairs(2, "far", [zz4, s3], [loss])
    near_coeffs = [v for k in range(4) for v in n[k][:2]]

    def text_dirs(name, coeffs, rule, span=None, us=2.2):
        outs = [shape(sum(r for _, r in spans), width) for spans in rule]
        start, stop = span or (0, coeffs[0].shape[1])
        return call(functools.partial(text_kernel, start, stop, rule), name, outs, [*coeffs, *lines], us=us)

    def image_dirs(k, rule, deps=(), us=2.2):
        outs = [shape(sum(r for _, r in spans), width) for spans in rule]
        ins = [*near_coeffs[2 * k : 2 * k + 2], *near, *mid_coeffs[2 * k : 2 * k + 2], *mid]
        ins += [*far_coeffs[2 * k : 2 * k + 2], *far]
        return call(functools.partial(image_kernel, rule), f"image{k}", outs, ins, deps, us=us)

    def add_loss(name, loss, flip):
        return gate(name, [[(8, [(loss, 0), (flip, 0)])]])[0]

    def add_loss(name, loss, flip, deps=()):
        return gate(name, [[(8, [(loss, 0), (flip, 0)])]], deps)[0]

    f = flipped(loss, 0)
    halves = [[(0, 2 * s)], [(2 * s, 2 * s)]]
    c_dn, c_up = image_dirs(3, [[(0, s), (2 * s, s)], [(s, s), (3 * s, s)]], us=U[0])
    c_dn, c_up = send(c_dn, down), send(c_up, up)
    p34, sw = text_dirs("text_far", far_coeffs, halves, us=U[1])
    s34 = send(sw, swap)
    loss = add_loss("loss1", loss, f)
    f = flipped(loss, 1)
    im1, ib1 = image_dirs(1, halves, us=U[2])
    loss = add_loss("loss2", loss, f)
    f = flipped(loss, 2)
    im2, ib2 = image_dirs(2, halves, us=U[3])
    loss = add_loss("loss3", loss, f)
    f = flipped(loss, 3)
    (z_out,) = gate("gate_q1", [[(2 * s, [(p34, 0), (s34, 0)])]])
    zq = send(z_out, back)
    p23, sw = text_dirs("text_mid", mid_coeffs, halves, us=U[4])
    s23 = send(sw, swap)
    t_12, sw = text_dirs("text_near", near_coeffs, [[(0, 2 * s)], [(2 * s, 3 * s)]], (3 * s, 8 * s), us=U[5])
    s12 = send(sw, swap)
    to_m, to_p, mine = call(
        fold_kernel,
        "fold",
        [shape(4 * s + 8, width)] * 2 + [shape(8, width)],
        [shards, loss, f, im1, ib1, im2, ib2, c_dn, c_up],
        special=1,
    )
    lm, lp, across = send(to_m, down), send(to_p, up), send(mine, second(2))
    (z_out,) = gate("gate_q2", [[(2 * s, [(p23, 0), (s23, 0), (zq, 0)])]])
    zq = send(z_out, back)
    t_o0, t_b0, t_o1 = text_dirs("text_own", near_coeffs, [[(0, s)], [(s, s)], [(2 * s, s)]], (0, 3 * s), us=U[6])
    im0, ib0 = image_dirs(0, halves, us=U[7])
    (z_out,) = gate("gate_q3", [[(2 * s, [(t_12, 0), (s12, s), (zq, 0)])]])
    zq = send(z_out, back)
    rows = (8, [(mine, 0), (lm, 4 * s), (lp, 4 * s), (across, 0)])
    own, e_fm, e_fp, e_f2 = gate(
        "gate_q4",
        [
            [(s, [(im0, 0), (lm, 0), (lp, 0)]), rows],
            [(s, [(im0, s), (lm, s), (lp, s)]), rows],
            [(s, [(ib0, 0), (lm, 2 * s), (lp, 2 * s)]), rows],
            [(s, [(ib0, s), (lm, 3 * s), (lp, 3 * s)]), rows],
        ],
    )
    em, ep, e2 = send(e_fm, first(-1)), send(e_fp, first(1)), send(e_f2, first(2))
    o_out, b_out = gate("gate_q5", [[(s, [(t_o1, 0), (s12, 0), (zq, s)])], [(s, [(t_b0, 0), (zq, 0)])]])
    zo, sb = send(o_out, back), send(b_out, swap)
    loss, image_grad, text_grad = call(
        last_kernel,
        "last",
        [jax.ShapeDtypeStruct((1,), F32)] + [shape(s, width)] * 2,
        [own, em, ep, e2, t_o0, zo, sb, images, texts],
        scratch=buffers,
        out_specs=(SMEM, VMEM, VMEM),
        raw=2,
    )
    return (loss, image_grad, text_grad)


def solution(mesh):
    return jax.shard_map(
        per_device,
        mesh=mesh,
        in_specs=(P(("wide", "narrow"), None), P(("narrow", "wide"), None), P(), P()),
        out_specs=(P(), P(("wide", "narrow"), None), P(("narrow", "wide"), None)),
        check_vma=False,
    )
```

```python
import functools

import jax
import jax.numpy as jnp
import numpy as np
from jax import lax
from jax.experimental import pallas as pl
from jax.experimental.pallas import tpu as pltpu
from jax.sharding import PartitionSpec as P

AXES = ("wide", "narrow")
BF = jnp.bfloat16
F32 = jnp.float32
ROWS = 64
BLOCK = 1024
TILE = 256
STEP = 32


def flat(x, y, z, c):
    x, y, z, c = x % 4, y % 4, z % 8, c % 2
    return ((x * 2 + z // 4) * 2 + c) * 16 + y * 4 + z % 4


PLACES = [(x, y, z, c) for x in range(4) for y in range(4) for z in range(8) for c in range(2)]


def table(move):
    return [(flat(*p), flat(*move(*p))) for p in PLACES]


def first_of(k, x, y, z, c):
    return (x + k, y, z, c) if c == 0 else (x, y + k, z, c)


def second_of(k, x, y, z, c):
    return (x, y + k, z, c) if c == 0 else (x + k, y, z, c)


def along_of(k, x, y, z, c):
    return (x, y, z + k, c) if c == 0 else (x, y, z - k, c)


def first(k):
    return table(functools.partial(first_of, k))


def second(k):
    return table(functools.partial(second_of, k))


def along(k):
    return table(functools.partial(along_of, k))


def sibling():
    return table(lambda x, y, z, c: (x, y, z, 1 - c))


def send(value, pairs):
    return lax.ppermute(value, AXES, pairs)


def cat(*parts):
    return jnp.concatenate(parts, axis=0)


LINE = (0, -1, 1, 2)
CHAIN_0 = [(0, 0), (0, 1), (1, 0), (1, 1), (2, 0)]
CHAIN_1 = [(1, 0), (1, 1), (2, 0)]
CHAIN_2 = [(2, 1), (3, 0)]
CHAIN_3 = [(3, 1), (4, 0)]
U = (2.2, 2.2, 8, 8, 1, 8, 4, 4)
GROUPS = (8 * ROWS, 4 * ROWS, 4 * ROWS)


def shard_tables():
    image = np.zeros((256, 17), np.int32)
    text = np.zeros((256, 16), np.int32)
    for place in PLACES:
        me = flat(*place)
        x, y, z, c = place
        image[me] = [flat(*first_of(k, *second_of(j, *place))) for j in LINE for k in LINE] + [x * 4 + y]

        def owner(at, k, sib):
            x, y, z, c = along_of(-k, *at)
            return flat(x, y, z, 1 - c if sib else c)

        twin = (x, y, z, 1 - c)
        held = [owner(place, k, sib) for k, sib in CHAIN_0] + [owner(twin, k, sib) for k, sib in CHAIN_1]
        for chain in (CHAIN_2, CHAIN_3):
            held += [owner(at, k, sib) for at in (place, twin) for k, sib in chain]
        text[me] = [(h % 16) * 16 + h // 16 for h in held]
    return image, text


IMAGE_SHARDS, TEXT_SHARDS = shard_tables()


FLIPS = [(0, 0, 4, 0), (0, 0, 2, 0), (0, 0, 1, 0), (0, 0, 0, 1)]


def flip_of(k, *at):
    return [a ^ b for a, b in zip(at, FLIPS[k])]


def flipped(value, k):
    return send(value, table(functools.partial(flip_of, k)))


def split(value):
    hi = value.astype(BF)
    return hi, (value - hi.astype(F32)).astype(BF)


def dot3(a_hi, a_lo, b_hi, b_lo, dims):
    def one(a, b):
        return lax.dot_general(a, b, (dims, ((), ())), preferred_element_type=F32)

    return one(a_hi, b_hi) + (one(a_hi, b_lo) + one(a_lo, b_hi))


def split_into(hi, lo, parts, spans):
    at = 0
    for p, start, count in spans:

        @pl.loop(0, count // 16)
        def _(i, part=parts[p], start=start, at=at):
            h, l = split(part[pl.ds(pl.multiple_of(start + i * 16, 16), 16), :])
            rows = pl.ds(pl.multiple_of(at + i * 16, 16), 16)
            hi[rows, :] = h
            lo[rows, :] = l

        at += count


def split_kernel(spans, *refs):
    split_into(refs[-2], refs[-1], refs[:-2], spans)


def coefficients(first_shard, rows, shards, params, col_ids, logits, c_hi, c_lo, acc):
    scale, shift = params[0], params[1]
    at = lax.broadcasted_iota(jnp.int32, (STEP, 1), 0)
    for i in range(rows // STEP):
        here = slice(i * STEP, (i + 1) * STEP)
        row_ids = shards[first_shard + i // (ROWS // STEP)] * ROWS + (i % (ROWS // STEP)) * STEP + at
        for c in range(0, logits.shape[1], 128):
            lanes = slice(c, c + 128)
            x = scale * logits[here, lanes] + shift
            same = row_ids == col_ids[:, lanes]
            e = jnp.exp(jnp.where(same, -x, x))
            p = 1.0 + e
            r = pl.reciprocal(p, approx=True)
            r = r * (2.0 - p * r)
            sig = e * r * scale
            h, l = split(jnp.where(same, -sig, sig))
            c_hi[here, lanes] = h
            c_lo[here, lanes] = l
            q = STEP // 4
            ea, eb, ec, ed = (e[j * q : (j + 1) * q, :] for j in range(4))
            u = ea + (eb + ea * eb)
            v = ec + (ed + ec * ed)
            acc = acc + jnp.log1p(u + (v + u * v))
    return acc


def near_kernel(k, spans, shards, params, col_ids, t_hi, t_lo, *refs):
    parts, (c_hi, c_lo, i_hi, i_lo, loss, logits) = refs[:-6], refs[-6:]
    split_into(i_hi, i_lo, parts, spans)
    acc = jnp.zeros((8, 128), F32)
    parts = []
    for c in range(0, logits.shape[1], 256):
        cols = slice(c, c + 256)
        logits[:, cols] = dot3(i_hi[...], i_lo[...], t_hi[cols, :], t_lo[cols, :], ((1,), (1,)))
        parts.append((k * 4, TILE, shards, params, col_ids.at[:, cols], logits.at[:, cols], c_hi.at[:, cols], c_lo.at[:, cols]))
    for part in parts:
        acc = coefficients(*part, acc)
    loss[...] = acc


def group_kernel(count, final, shards, params, col_ids, *refs):
    lines, parts, losses = refs[:8], refs[8:10], refs[10 : 10 + count]
    stores, (t_hi, t_lo, loss, logits) = refs[10 + count : 18 + count], refs[18 + count :]
    split_into(t_hi, t_lo, parts, [(0, 0, parts[0].shape[0]), (1, 0, parts[1].shape[0])])
    acc = jnp.zeros((8, 128), F32)
    for k in range(4):
        rows = slice(k * TILE, (k + 1) * TILE)
        logits[rows, :] = dot3(lines[2 * k][...], lines[2 * k + 1][...], t_hi[...], t_lo[...], ((1,), (1,)))
        if k:
            acc = coefficients(4 * k - 4, TILE, shards, params, col_ids, logits.at[last, :], stores[2 * k - 2], stores[2 * k - 1], acc)
        last = rows
    acc = coefficients(12, TILE, shards, params, col_ids, logits.at[last, :], stores[6], stores[7], acc)
    for part in losses:
        acc = acc + part[...]
    loss[...] = jnp.full(loss.shape, jnp.sum(acc), F32) if final else acc


def fold_kernel(shards, loss, flip, am, bm, ap, bp, down, up, to_m, to_p, mine):
    s = ROWS
    total = (loss[...] + flip[...])[:1, :1]
    row = lax.broadcasted_iota(jnp.int32, mine.shape, 0)
    lane = lax.broadcasted_iota(jnp.int32, mine.shape, 1)
    value = jnp.where((row == 0) & (lane == shards[16]), total, 0.0)
    mine[...] = value
    to_m[:s, :] = am[:s, :] + down[:s, :]
    to_m[s : 2 * s, :] = am[s:, :]
    to_m[2 * s : 3 * s, :] = bm[:s, :] + down[s:, :]
    to_m[3 * s : 4 * s, :] = bm[s:, :]
    to_m[4 * s :, :] = value
    to_p[:s, :] = ap[:s, :]
    to_p[s : 2 * s, :] = ap[s:, :] + up[:s, :]
    to_p[2 * s : 3 * s, :] = bp[:s, :]
    to_p[3 * s : 4 * s, :] = bp[s:, :] + up[s:, :]
    to_p[4 * s :, :] = value


def gate_kernel(count, rule, *refs):
    ins, outs = refs[:count], refs[count:]
    for out, pieces in zip(outs, rule):
        at = 0
        for rows, terms in pieces:
            total = None
            for p, start in terms:
                v = ins[p][start : start + rows, :]
                total = v if total is None else total + v
            out[at : at + rows, :] = total
            at += rows


def store(outs, rule, value):
    for out, spans in zip(outs, rule):
        at = 0
        for start, rows in spans:
            out[at : at + rows, :] = value[start : start + rows, :]
            at += rows


def image_kernel(rule, *refs):
    ins, outs = refs[:12], refs[12:]
    total = None
    for g in range(3):
        d = dot3(*(r[...] for r in ins[4 * g : 4 * g + 4]), ((1,), (0,)))
        total = d if total is None else total + d
    store(outs, rule, total)


def text_kernel(start, stop, rule, *refs):
    ins, outs = refs[:16], refs[16:]
    total = None
    for k in range(4):
        c_hi, c_lo = (r[:, start:stop] for r in ins[2 * k : 2 * k + 2])
        d = dot3(c_hi, c_lo, ins[8 + 2 * k][...], ins[9 + 2 * k][...], ((0,), (0,)))
        total = d if total is None else total + d
    store(outs, rule, total)


VMEM = pl.BlockSpec(memory_space=pltpu.VMEM)
SMEM = pl.BlockSpec(memory_space=pltpu.SMEM)


def unit_kernel(images, texts, iu, tu, x, y, sems):
    copies = [pltpu.make_async_copy(a, b, sems.at[i]) for i, (a, b) in enumerate(((images, x), (texts, y)))]
    for copy in copies:
        copy.start()
    for copy, source, out in zip(copies, (x, y), (iu, tu)):
        copy.wait()
        v = source[...]
        out[...] = v / jnp.sqrt(jnp.sum(v * v, axis=1, keepdims=True) + 1e-06)


def project(parts, source, out):
    d = parts[0]
    for part in parts[1:]:
        d = d + part
    x = source[...]
    norm = jnp.sqrt(jnp.sum(x * x, axis=1, keepdims=True) + 1e-06)
    u = x / norm
    out[...] = (d - u * jnp.sum(d * u, axis=1, keepdims=True)) / norm


def last_kernel(own, em, ep, e2, o0, zo, sb, images, texts, loss, image_grad, text_grad, x, y, sems):
    s = ROWS
    copies = [pltpu.make_async_copy(a, b, sems.at[i]) for i, (a, b) in enumerate(((images, x), (texts, y)))]
    for copy in copies:
        copy.start()
    for copy in copies:
        copy.wait()
    project([own[:s, :], em[:s, :], ep[:s, :], e2[:s, :]], x, image_grad)
    project([o0[...], zo[...], sb[...]], y, text_grad)
    rows = own[s:, :] + em[s:, :] + ep[s:, :] + e2[s:, :]
    loss[0] = jnp.sum(rows) / 16384.0


def shape(rows, cols, dtype=F32):
    return jax.ShapeDtypeStruct((rows, cols), dtype)


class Chain:
    def __init__(self):
        self.token = None

    def call(self, kernel, name, outs, ins, deps=(), scratch=(), vmem=16, special=0, out_specs=None, raw=0, us=0.1):
        outs, ins, deps = tuple(outs), list(ins), list(deps)
        if self.token is not None and not any(self.token is v for v in ins + deps):
            deps.append(self.token)
        count = len(ins)
        anywhere = pl.BlockSpec(memory_space=pl.ANY)

        def body(*refs):
            kernel(*refs[:count], *refs[count + len(deps) :])

        out = pl.pallas_call(
            body,
            out_shape=outs,
            in_specs=[SMEM] * special + [VMEM] * (count - special - raw) + [pl.BlockSpec(memory_space=pltpu.HBM)] * raw + [anywhere] * len(deps),
            out_specs=out_specs or (VMEM,) * len(outs),
            scratch_shapes=scratch,
            compiler_params=pltpu.CompilerParams(vmem_limit_bytes=vmem << 20),
            cost_estimate=pl.CostEstimate(flops=int(us * 1e9), bytes_accessed=1 << 16, transcendentals=0),
            name=name,
        )(*ins, *deps)
        self.token = out[-1]
        return out

    def gate(self, name, rule, deps=()):
        ins = []

        def place(array):
            for i, known in enumerate(ins):
                if known is array:
                    return i
            ins.append(array)
            return len(ins) - 1

        rule = [[(rows, [(place(v), start) for v, start in terms]) for rows, terms in pieces] for pieces in rule]
        outs = [shape(sum(rows for rows, _ in pieces), ins[pieces[0][1][0][0]].shape[1]) for pieces in rule]
        return self.call(functools.partial(gate_kernel, len(ins), rule), name, outs, ins, deps)


def per_device(images, texts, log_scale, bias):
    width = images.shape[1]
    s = ROWS
    me = lax.axis_index("wide") * 16 + lax.axis_index("narrow")
    shards = lax.dynamic_index_in_dim(jnp.asarray(IMAGE_SHARDS), me, 0, keepdims=False)
    text_shards = lax.dynamic_index_in_dim(jnp.asarray(TEXT_SHARDS), me, 0, keepdims=False)
    col_ids = (text_shards[:, None] * ROWS + jnp.arange(ROWS, dtype=jnp.int32)).reshape(1, BLOCK)
    params = jnp.concatenate([jnp.exp(log_scale), bias])
    ids = [col_ids[:, : 8 * s], col_ids[:, 8 * s : 12 * s], col_ids[:, 12 * s :]]
    swap, ahead, back = sibling(), along(1), along(-1)
    up, down = second(1), second(-1)
    chain = Chain()
    call, gate = chain.call, chain.gate

    def copy(rows, *pieces):
        return [(r, [(v, start)]) for r, (v, start) in zip(rows, pieces)]

    buffers = [pltpu.VMEM((s, width), F32)] * 2 + [pltpu.SemaphoreType.DMA((2,))]
    iu, tu = call(unit_kernel, "units", [shape(s, width)] * 2, [images, texts], scratch=buffers, raw=2)
    fm, fp, f2 = send(iu, first(1)), send(iu, first(-1)), send(iu, first(2))
    o1, b0 = send(tu, ahead), send(tu, swap)
    (zb,) = gate("gate_z1", [copy((s, s), (b0, 0), (o1, 0))])
    z2 = send(zb, ahead)
    (l0,) = gate("gate_l", [copy((s, s, s, s), (iu, 0), (fm, 0), (fp, 0), (f2, 0))])
    lm, lp = send(l0, up), send(l0, down)
    zz2, sw1 = gate("gate_z2", [copy((2 * s,), (z2, 0)), copy((s, 2 * s), (o1, 0), (z2, 0))], [shards, params, *ids])
    z3, s1 = send(zz2, ahead), send(sw1, swap)
    near = call(
        functools.partial(split_kernel, [(0, 0, s), (1, 0, s), (2, 0, s), (3, 0, 2 * s), (4, 0, 3 * s)]),
        "split_near",
        [shape(8 * s, width, BF)] * 2,
        [tu, b0, o1, zz2, s1],
    )

    def near_pairs(k, parts, spans):
        return call(
            functools.partial(near_kernel, k, spans),
            f"near{k}",
            [shape(TILE, GROUPS[0], BF)] * 2 + [shape(TILE, width, BF)] * 2 + [shape(8, 128)],
            [shards, params, ids[0], *near, *parts],
            scratch=[pltpu.VMEM((TILE, GROUPS[0]), F32)],
            special=2,
            us=2.5,
        )

    one = [(0, 0, 4 * s)]
    n0 = near_pairs(0, [l0], one)
    (zz3,) = gate("gate_z3", [copy((2 * s,), (z3, 0))])
    z4, s2 = send(zz3, ahead), send(zz3, swap)
    cu, cd = gate("gate_c", [copy((s, s), (lm, 0), (lm, 2 * s)), copy((s, s), (lp, s), (lp, 3 * s))])
    cu, cd = send(cu, up), send(cd, down)
    n1 = near_pairs(1, [lm], one)
    n2 = near_pairs(2, [lp], one)
    (zz4,) = gate("gate_z4", [copy((2 * s,), (z4, 0))])
    s3 = send(zz4, swap)
    n3 = near_pairs(3, [cu, cd], [(0, 0, s), (1, 0, s), (0, s, s), (1, s, s)])
    n = [n0, n1, n2, n3]
    lines = [v for k in range(4) for v in n[k][2:4]]

    def group_pairs(g, name, parts, losses):
        out = call(
            functools.partial(group_kernel, len(losses), g == 2),
            name,
            [shape(TILE, GROUPS[g], BF)] * 8 + [shape(GROUPS[g], width, BF)] * 2 + [shape(8, 128)],
            [shards, params, ids[g], *lines, *parts, *losses],
            scratch=[pltpu.VMEM((BLOCK, GROUPS[g]), F32)],
            special=2,
            us=4.5,
        )
        return out[:8], out[8:10], out[10]

    mid_coeffs, mid, loss = group_pairs(1, "mid", [zz3, s2], [n[k][4] for k in range(4)])
    far_coeffs, far, loss = group_pairs(2, "far", [zz4, s3], [loss])
    near_coeffs = [v for k in range(4) for v in n[k][:2]]

    def text_dirs(name, coeffs, rule, span=None, us=2.2):
        outs = [shape(sum(r for _, r in spans), width) for spans in rule]
        start, stop = span or (0, coeffs[0].shape[1])
        return call(functools.partial(text_kernel, start, stop, rule), name, outs, [*coeffs, *lines], us=us)

    def image_dirs(k, rule, deps=(), us=2.2):
        outs = [shape(sum(r for _, r in spans), width) for spans in rule]
        ins = [*near_coeffs[2 * k : 2 * k + 2], *near, *mid_coeffs[2 * k : 2 * k + 2], *mid]
        ins += [*far_coeffs[2 * k : 2 * k + 2], *far]
        return call(functools.partial(image_kernel, rule), f"image{k}", outs, ins, deps, us=us)

    def add_loss(name, loss, flip):
        return gate(name, [[(8, [(loss, 0), (flip, 0)])]])[0]

    def add_loss(name, loss, flip, deps=()):
        return gate(name, [[(8, [(loss, 0), (flip, 0)])]], deps)[0]

    f = flipped(loss, 0)
    halves = [[(0, 2 * s)], [(2 * s, 2 * s)]]
    c_dn, c_up = image_dirs(3, [[(0, s), (2 * s, s)], [(s, s), (3 * s, s)]], us=U[0])
    c_dn, c_up = send(c_dn, down), send(c_up, up)
    p34, sw = text_dirs("text_far", far_coeffs, halves, us=U[1])
    s34 = send(sw, swap)
    loss = add_loss("loss1", loss, f)
    f = flipped(loss, 1)
    im1, ib1 = image_dirs(1, halves, us=U[2])
    loss = add_loss("loss2", loss, f)
    f = flipped(loss, 2)
    im2, ib2 = image_dirs(2, halves, us=U[3])
    loss = add_loss("loss3", loss, f)
    f = flipped(loss, 3)
    (z_out,) = gate("gate_q1", [[(2 * s, [(p34, 0), (s34, 0)])]])
    zq = send(z_out, back)
    p23, sw = text_dirs("text_mid", mid_coeffs, halves, us=U[4])
    s23 = send(sw, swap)
    t_12, sw = text_dirs("text_near", near_coeffs, [[(0, 2 * s)], [(2 * s, 3 * s)]], (3 * s, 8 * s), us=U[5])
    s12 = send(sw, swap)
    to_m, to_p, mine = call(
        fold_kernel,
        "fold",
        [shape(4 * s + 8, width)] * 2 + [shape(8, width)],
        [shards, loss, f, im1, ib1, im2, ib2, c_dn, c_up],
        special=1,
    )
    lm, lp, across = send(to_m, down), send(to_p, up), send(mine, second(2))
    (z_out,) = gate("gate_q2", [[(2 * s, [(p23, 0), (s23, 0), (zq, 0)])]])
    zq = send(z_out, back)
    t_o0, t_b0, t_o1 = text_dirs("text_own", near_coeffs, [[(0, s)], [(s, s)], [(2 * s, s)]], (0, 3 * s), us=U[6])
    im0, ib0 = image_dirs(0, halves, us=U[7])
    (z_out,) = gate("gate_q3", [[(2 * s, [(t_12, 0), (s12, s), (zq, 0)])]])
    zq = send(z_out, back)
    rows = (8, [(mine, 0), (lm, 4 * s), (lp, 4 * s), (across, 0)])
    own, e_fm, e_fp, e_f2 = gate(
        "gate_q4",
        [
            [(s, [(im0, 0), (lm, 0), (lp, 0)]), rows],
            [(s, [(im0, s), (lm, s), (lp, s)]), rows],
            [(s, [(ib0, 0), (lm, 2 * s), (lp, 2 * s)]), rows],
            [(s, [(ib0, s), (lm, 3 * s), (lp, 3 * s)]), rows],
        ],
    )
    em, ep, e2 = send(e_fm, first(-1)), send(e_fp, first(1)), send(e_f2, first(2))
    o_out, b_out = gate("gate_q5", [[(s, [(t_o1, 0), (s12, 0), (zq, s)])], [(s, [(t_b0, 0), (zq, 0)])]])
    zo, sb = send(o_out, back), send(b_out, swap)
    loss, image_grad, text_grad = call(
        last_kernel,
        "last",
        [jax.ShapeDtypeStruct((1,), F32)] + [shape(s, width)] * 2,
        [own, em, ep, e2, t_o0, zo, sb, images, texts],
        scratch=buffers,
        out_specs=(SMEM, VMEM, VMEM),
        raw=2,
    )
    return (loss, image_grad, text_grad)


def solution(mesh):
    return jax.shard_map(
        per_device,
        mesh=mesh,
        in_specs=(P(("wide", "narrow"), None), P(("narrow", "wide"), None), P(), P()),
        out_specs=(P(), P(("wide", "narrow"), None), P(("narrow", "wide"), None)),
        check_vma=False,
    )
```

```python
import functools

import jax
import jax.numpy as jnp
import numpy as np
from jax import lax
from jax.experimental import pallas as pl
from jax.experimental.pallas import tpu as pltpu
from jax.sharding import PartitionSpec as P

AXES = ("wide", "narrow")
BF = jnp.bfloat16
F32 = jnp.float32
ROWS = 64
BLOCK = 1024
TILE = 256
STEP = 32


def flat(x, y, z, c):
    x, y, z, c = x % 4, y % 4, z % 8, c % 2
    return ((x * 2 + z // 4) * 2 + c) * 16 + y * 4 + z % 4


PLACES = [(x, y, z, c) for x in range(4) for y in range(4) for z in range(8) for c in range(2)]


def table(move):
    return [(flat(*p), flat(*move(*p))) for p in PLACES]


def first_of(k, x, y, z, c):
    return (x + k, y, z, c) if c == 0 else (x, y + k, z, c)


def second_of(k, x, y, z, c):
    return (x, y + k, z, c) if c == 0 else (x + k, y, z, c)


def along_of(k, x, y, z, c):
    return (x, y, z + k, c) if c == 0 else (x, y, z - k, c)


def first(k):
    return table(functools.partial(first_of, k))


def second(k):
    return table(functools.partial(second_of, k))


def along(k):
    return table(functools.partial(along_of, k))


def sibling():
    return table(lambda x, y, z, c: (x, y, z, 1 - c))


def send(value, pairs):
    return lax.ppermute(value, AXES, pairs)


def cat(*parts):
    return jnp.concatenate(parts, axis=0)


LINE = (0, -1, 1, 2)
CHAIN_0 = [(0, 0), (0, 1), (1, 0), (1, 1), (2, 0)]
CHAIN_1 = [(1, 0), (1, 1), (2, 0)]
CHAIN_2 = [(2, 1), (3, 0)]
CHAIN_3 = [(3, 1), (4, 0)]
U = (2.2, 2.2, 8, 8, 1, 8, 4, 4)
GROUPS = (8 * ROWS, 4 * ROWS, 4 * ROWS)


def shard_tables():
    image = np.zeros((256, 17), np.int32)
    text = np.zeros((256, 16), np.int32)
    for place in PLACES:
        me = flat(*place)
        x, y, z, c = place
        image[me] = [flat(*first_of(k, *second_of(j, *place))) for j in LINE for k in LINE] + [x * 4 + y]

        def owner(at, k, sib):
            x, y, z, c = along_of(-k, *at)
            return flat(x, y, z, 1 - c if sib else c)

        twin = (x, y, z, 1 - c)
        held = [owner(place, k, sib) for k, sib in CHAIN_0] + [owner(twin, k, sib) for k, sib in CHAIN_1]
        for chain in (CHAIN_2, CHAIN_3):
            held += [owner(at, k, sib) for at in (place, twin) for k, sib in chain]
        text[me] = [(h % 16) * 16 + h // 16 for h in held]
    return image, text


IMAGE_SHARDS, TEXT_SHARDS = shard_tables()


FLIPS = [(0, 0, 4, 0), (0, 0, 2, 0), (0, 0, 1, 0), (0, 0, 0, 1)]


def flip_of(k, *at):
    return [a ^ b for a, b in zip(at, FLIPS[k])]


def flipped(value, k):
    return send(value, table(functools.partial(flip_of, k)))


def split(value):
    hi = value.astype(BF)
    return hi, (value - hi.astype(F32)).astype(BF)


def dot3(a_hi, a_lo, b_hi, b_lo, dims):
    def one(a, b):
        return lax.dot_general(a, b, (dims, ((), ())), preferred_element_type=F32)

    return one(a_hi, b_hi) + (one(a_hi, b_lo) + one(a_lo, b_hi))


def split_into(hi, lo, parts, spans):
    at = 0
    for p, start, count in spans:

        @pl.loop(0, count // 16, unroll=4)
        def _(i, part=parts[p], start=start, at=at):
            h, l = split(part[pl.ds(pl.multiple_of(start + i * 16, 16), 16), :])
            rows = pl.ds(pl.multiple_of(at + i * 16, 16), 16)
            hi[rows, :] = h
            lo[rows, :] = l

        at += count


def split_kernel(spans, *refs):
    split_into(refs[-2], refs[-1], refs[:-2], spans)


def coefficients(first_shard, rows, shards, params, col_ids, logits, c_hi, c_lo, acc):
    scale, shift = params[0], params[1]
    at = lax.broadcasted_iota(jnp.int32, (STEP, 1), 0)
    for i in range(rows // STEP):
        here = slice(i * STEP, (i + 1) * STEP)
        row_ids = shards[first_shard + i // (ROWS // STEP)] * ROWS + (i % (ROWS // STEP)) * STEP + at
        for c in range(0, logits.shape[1], 128):
            lanes = slice(c, c + 128)
            x = scale * logits[here, lanes] + shift
            same = row_ids == col_ids[:, lanes]
            e = jnp.exp(jnp.where(same, -x, x))
            p = 1.0 + e
            r = pl.reciprocal(p, approx=True)
            r = r * (2.0 - p * r)
            sig = e * r * scale
            h, l = split(jnp.where(same, -sig, sig))
            c_hi[here, lanes] = h
            c_lo[here, lanes] = l
            q = STEP // 4
            ea, eb, ec, ed = (e[j * q : (j + 1) * q, :] for j in range(4))
            u = ea + (eb + ea * eb)
            v = ec + (ed + ec * ed)
            acc = acc + jnp.log1p(u + (v + u * v))
    return acc


def near_kernel(k, spans, shards, params, col_ids, t_hi, t_lo, *refs):
    parts, (c_hi, c_lo, i_hi, i_lo, loss, logits) = refs[:-6], refs[-6:]
    split_into(i_hi, i_lo, parts, spans)
    acc = jnp.zeros((8, 128), F32)
    parts = []
    for c in range(0, logits.shape[1], 256):
        cols = slice(c, c + 256)
        logits[:, cols] = dot3(i_hi[...], i_lo[...], t_hi[cols, :], t_lo[cols, :], ((1,), (1,)))
        parts.append((k * 4, TILE, shards, params, col_ids.at[:, cols], logits.at[:, cols], c_hi.at[:, cols], c_lo.at[:, cols]))
    for part in parts:
        acc = coefficients(*part, acc)
    loss[...] = acc


def group_kernel(count, final, shards, params, col_ids, *refs):
    lines, parts, losses = refs[:8], refs[8:10], refs[10 : 10 + count]
    stores, (t_hi, t_lo, loss, logits) = refs[10 + count : 18 + count], refs[18 + count :]
    split_into(t_hi, t_lo, parts, [(0, 0, parts[0].shape[0]), (1, 0, parts[1].shape[0])])
    acc = jnp.zeros((8, 128), F32)
    for k in range(4):
        rows = slice(k * TILE, (k + 1) * TILE)
        logits[rows, :] = dot3(lines[2 * k][...], lines[2 * k + 1][...], t_hi[...], t_lo[...], ((1,), (1,)))
        if k:
            acc = coefficients(4 * k - 4, TILE, shards, params, col_ids, logits.at[last, :], stores[2 * k - 2], stores[2 * k - 1], acc)
        last = rows
    acc = coefficients(12, TILE, shards, params, col_ids, logits.at[last, :], stores[6], stores[7], acc)
    for part in losses:
        acc = acc + part[...]
    loss[...] = jnp.full(loss.shape, jnp.sum(acc), F32) if final else acc


def fold_kernel(shards, loss, flip, am, bm, ap, bp, down, up, to_m, to_p, mine):
    s = ROWS
    total = (loss[...] + flip[...])[:1, :1]
    row = lax.broadcasted_iota(jnp.int32, mine.shape, 0)
    lane = lax.broadcasted_iota(jnp.int32, mine.shape, 1)
    value = jnp.where((row == 0) & (lane == shards[16]), total, 0.0)
    mine[...] = value
    to_m[:s, :] = am[:s, :] + down[:s, :]
    to_m[s : 2 * s, :] = am[s:, :]
    to_m[2 * s : 3 * s, :] = bm[:s, :] + down[s:, :]
    to_m[3 * s : 4 * s, :] = bm[s:, :]
    to_m[4 * s :, :] = value
    to_p[:s, :] = ap[:s, :]
    to_p[s : 2 * s, :] = ap[s:, :] + up[:s, :]
    to_p[2 * s : 3 * s, :] = bp[:s, :]
    to_p[3 * s : 4 * s, :] = bp[s:, :] + up[s:, :]
    to_p[4 * s :, :] = value


def gate_kernel(count, rule, *refs):
    ins, outs = refs[:count], refs[count:]
    for out, pieces in zip(outs, rule):
        at = 0
        for rows, terms in pieces:
            total = None
            for p, start in terms:
                v = ins[p][start : start + rows, :]
                total = v if total is None else total + v
            out[at : at + rows, :] = total
            at += rows


def store(outs, rule, value):
    for out, spans in zip(outs, rule):
        at = 0
        for start, rows in spans:
            out[at : at + rows, :] = value[start : start + rows, :]
            at += rows


def image_kernel(rule, *refs):
    ins, outs = refs[:12], refs[12:]
    total = None
    for g in range(3):
        d = dot3(*(r[...] for r in ins[4 * g : 4 * g + 4]), ((1,), (0,)))
        total = d if total is None else total + d
    store(outs, rule, total)


def text_kernel(start, stop, rule, *refs):
    ins, outs = refs[:16], refs[16:]
    total = None
    for k in range(4):
        c_hi, c_lo = (r[:, start:stop] for r in ins[2 * k : 2 * k + 2])
        d = dot3(c_hi, c_lo, ins[8 + 2 * k][...], ins[9 + 2 * k][...], ((0,), (0,)))
        total = d if total is None else total + d
    store(outs, rule, total)


VMEM = pl.BlockSpec(memory_space=pltpu.VMEM)
SMEM = pl.BlockSpec(memory_space=pltpu.SMEM)


def unit_kernel(source, out):
    v = source[...]
    out[...] = v / jnp.sqrt(jnp.sum(v * v, axis=1, keepdims=True) + 1e-06)


def project(parts, source, out):
    d = parts[0]
    for part in parts[1:]:
        d = d + part
    x = source[...]
    norm = jnp.sqrt(jnp.sum(x * x, axis=1, keepdims=True) + 1e-06)
    u = x / norm
    out[...] = (d - u * jnp.sum(d * u, axis=1, keepdims=True)) / norm


def last_kernel(own, em, ep, e2, o0, zo, sb, images, texts, loss, image_grad, text_grad):
    s = ROWS
    project([own[:s, :], em[:s, :], ep[:s, :], e2[:s, :]], images, image_grad)
    project([o0[...], zo[...], sb[...]], texts, text_grad)
    rows = own[s:, :] + em[s:, :] + ep[s:, :] + e2[s:, :]
    loss[0] = jnp.sum(rows) / 16384.0


def shape(rows, cols, dtype=F32):
    return jax.ShapeDtypeStruct((rows, cols), dtype)


class Chain:
    def __init__(self):
        self.token = None

    def call(self, kernel, name, outs, ins, deps=(), scratch=(), vmem=16, special=0, out_specs=None, raw=0, us=0.1):
        outs, ins, deps = tuple(outs), list(ins), list(deps)
        if self.token is not None and not any(self.token is v for v in ins + deps):
            deps.append(self.token)
        count = len(ins)
        anywhere = pl.BlockSpec(memory_space=pl.ANY)

        def body(*refs):
            kernel(*refs[:count], *refs[count + len(deps) :])

        out = pl.pallas_call(
            body,
            out_shape=outs,
            in_specs=[SMEM] * special + [VMEM] * (count - special - raw) + [pl.BlockSpec(memory_space=pltpu.HBM)] * raw + [anywhere] * len(deps),
            out_specs=out_specs or (VMEM,) * len(outs),
            scratch_shapes=scratch,
            compiler_params=pltpu.CompilerParams(vmem_limit_bytes=vmem << 20),
            cost_estimate=pl.CostEstimate(flops=int(us * 1e9), bytes_accessed=1 << 16, transcendentals=0),
            name=name,
        )(*ins, *deps)
        self.token = out[-1]
        return out

    def gate(self, name, rule, deps=()):
        ins = []

        def place(array):
            for i, known in enumerate(ins):
                if known is array:
                    return i
            ins.append(array)
            return len(ins) - 1

        rule = [[(rows, [(place(v), start) for v, start in terms]) for rows, terms in pieces] for pieces in rule]
        outs = [shape(sum(rows for rows, _ in pieces), ins[pieces[0][1][0][0]].shape[1]) for pieces in rule]
        return self.call(functools.partial(gate_kernel, len(ins), rule), name, outs, ins, deps)


def per_device(images, texts, log_scale, bias):
    width = images.shape[1]
    s = ROWS
    me = lax.axis_index("wide") * 16 + lax.axis_index("narrow")
    shards = lax.dynamic_index_in_dim(jnp.asarray(IMAGE_SHARDS), me, 0, keepdims=False)
    text_shards = lax.dynamic_index_in_dim(jnp.asarray(TEXT_SHARDS), me, 0, keepdims=False)
    col_ids = (text_shards[:, None] * ROWS + jnp.arange(ROWS, dtype=jnp.int32)).reshape(1, BLOCK)
    params = jnp.concatenate([jnp.exp(log_scale), bias])
    ids = [col_ids[:, : 8 * s], col_ids[:, 8 * s : 12 * s], col_ids[:, 12 * s :]]
    swap, ahead, back = sibling(), along(1), along(-1)
    up, down = second(1), second(-1)
    chain = Chain()
    call, gate = chain.call, chain.gate

    def copy(rows, *pieces):
        return [(r, [(v, start)]) for r, (v, start) in zip(rows, pieces)]

    (tu,) = call(unit_kernel, "text_units", [shape(s, width)], [texts])
    (iu,) = call(unit_kernel, "image_units", [shape(s, width)], [images])
    fm, fp, f2 = send(iu, first(1)), send(iu, first(-1)), send(iu, first(2))
    o1, b0 = send(tu, ahead), send(tu, swap)
    (zb,) = gate("gate_z1", [copy((s, s), (b0, 0), (o1, 0))])
    z2 = send(zb, ahead)
    (l0,) = gate("gate_l", [copy((s, s, s, s), (iu, 0), (fm, 0), (fp, 0), (f2, 0))])
    lm, lp = send(l0, up), send(l0, down)
    zz2, sw1 = gate("gate_z2", [copy((2 * s,), (z2, 0)), copy((s, 2 * s), (o1, 0), (z2, 0))], [shards, params, *ids])
    z3, s1 = send(zz2, ahead), send(sw1, swap)
    near = call(
        functools.partial(split_kernel, [(0, 0, s), (1, 0, s), (2, 0, s), (3, 0, 2 * s), (4, 0, 3 * s)]),
        "split_near",
        [shape(8 * s, width, BF)] * 2,
        [tu, b0, o1, zz2, s1],
    )

    def near_pairs(k, parts, spans):
        return call(
            functools.partial(near_kernel, k, spans),
            f"near{k}",
            [shape(TILE, GROUPS[0], BF)] * 2 + [shape(TILE, width, BF)] * 2 + [shape(8, 128)],
            [shards, params, ids[0], *near, *parts],
            scratch=[pltpu.VMEM((TILE, GROUPS[0]), F32)],
            special=2,
            us=2.5,
        )

    one = [(0, 0, 4 * s)]
    n0 = near_pairs(0, [l0], one)
    (zz3,) = gate("gate_z3", [copy((2 * s,), (z3, 0))])
    z4, s2 = send(zz3, ahead), send(zz3, swap)
    cu, cd = gate("gate_c", [copy((s, s), (lm, 0), (lm, 2 * s)), copy((s, s), (lp, s), (lp, 3 * s))])
    cu, cd = send(cu, up), send(cd, down)
    n1 = near_pairs(1, [lm], one)
    n2 = near_pairs(2, [lp], one)
    (zz4,) = gate("gate_z4", [copy((2 * s,), (z4, 0))])
    s3 = send(zz4, swap)
    n3 = near_pairs(3, [cu, cd], [(0, 0, s), (1, 0, s), (0, s, s), (1, s, s)])
    n = [n0, n1, n2, n3]
    lines = [v for k in range(4) for v in n[k][2:4]]

    def group_pairs(g, name, parts, losses):
        out = call(
            functools.partial(group_kernel, len(losses), g == 2),
            name,
            [shape(TILE, GROUPS[g], BF)] * 8 + [shape(GROUPS[g], width, BF)] * 2 + [shape(8, 128)],
            [shards, params, ids[g], *lines, *parts, *losses],
            scratch=[pltpu.VMEM((BLOCK, GROUPS[g]), F32)],
            special=2,
            us=4.5,
        )
        return out[:8], out[8:10], out[10]

    mid_coeffs, mid, loss = group_pairs(1, "mid", [zz3, s2], [n[k][4] for k in range(4)])
    far_coeffs, far, loss = group_pairs(2, "far", [zz4, s3], [loss])
    near_coeffs = [v for k in range(4) for v in n[k][:2]]

    def text_dirs(name, coeffs, rule, span=None, us=2.2):
        outs = [shape(sum(r for _, r in spans), width) for spans in rule]
        start, stop = span or (0, coeffs[0].shape[1])
        return call(functools.partial(text_kernel, start, stop, rule), name, outs, [*coeffs, *lines], us=us)

    def image_dirs(k, rule, deps=(), us=2.2):
        outs = [shape(sum(r for _, r in spans), width) for spans in rule]
        ins = [*near_coeffs[2 * k : 2 * k + 2], *near, *mid_coeffs[2 * k : 2 * k + 2], *mid]
        ins += [*far_coeffs[2 * k : 2 * k + 2], *far]
        return call(functools.partial(image_kernel, rule), f"image{k}", outs, ins, deps, us=us)

    def add_loss(name, loss, flip):
        return gate(name, [[(8, [(loss, 0), (flip, 0)])]])[0]

    def add_loss(name, loss, flip, deps=()):
        return gate(name, [[(8, [(loss, 0), (flip, 0)])]], deps)[0]

    f = flipped(loss, 0)
    halves = [[(0, 2 * s)], [(2 * s, 2 * s)]]
    c_dn, c_up = image_dirs(3, [[(0, s), (2 * s, s)], [(s, s), (3 * s, s)]], us=U[0])
    c_dn, c_up = send(c_dn, down), send(c_up, up)
    p34, sw = text_dirs("text_far", far_coeffs, halves, us=U[1])
    s34 = send(sw, swap)
    loss = add_loss("loss1", loss, f)
    f = flipped(loss, 1)
    im1, ib1 = image_dirs(1, halves, us=U[2])
    loss = add_loss("loss2", loss, f)
    f = flipped(loss, 2)
    im2, ib2 = image_dirs(2, halves, us=U[3])
    loss = add_loss("loss3", loss, f)
    f = flipped(loss, 3)
    (z_out,) = gate("gate_q1", [[(2 * s, [(p34, 0), (s34, 0)])]])
    zq = send(z_out, back)
    p23, sw = text_dirs("text_mid", mid_coeffs, halves, us=U[4])
    s23 = send(sw, swap)
    t_12, sw = text_dirs("text_near", near_coeffs, [[(0, 2 * s)], [(2 * s, 3 * s)]], (3 * s, 8 * s), us=U[5])
    s12 = send(sw, swap)
    to_m, to_p, mine = call(
        fold_kernel,
        "fold",
        [shape(4 * s + 8, width)] * 2 + [shape(8, width)],
        [shards, loss, f, im1, ib1, im2, ib2, c_dn, c_up],
        special=1,
    )
    lm, lp, across = send(to_m, down), send(to_p, up), send(mine, second(2))
    (z_out,) = gate("gate_q2", [[(2 * s, [(p23, 0), (s23, 0), (zq, 0)])]])
    zq = send(z_out, back)
    t_o0, t_b0, t_o1 = text_dirs("text_own", near_coeffs, [[(0, s)], [(s, s)], [(2 * s, s)]], (0, 3 * s), us=U[6])
    im0, ib0 = image_dirs(0, halves, us=U[7])
    (z_out,) = gate("gate_q3", [[(2 * s, [(t_12, 0), (s12, s), (zq, 0)])]])
    zq = send(z_out, back)
    rows = (8, [(mine, 0), (lm, 4 * s), (lp, 4 * s), (across, 0)])
    own, e_fm, e_fp, e_f2 = gate(
        "gate_q4",
        [
            [(s, [(im0, 0), (lm, 0), (lp, 0)]), rows],
            [(s, [(im0, s), (lm, s), (lp, s)]), rows],
            [(s, [(ib0, 0), (lm, 2 * s), (lp, 2 * s)]), rows],
            [(s, [(ib0, s), (lm, 3 * s), (lp, 3 * s)]), rows],
        ],
    )
    em, ep, e2 = send(e_fm, first(-1)), send(e_fp, first(1)), send(e_f2, first(2))
    o_out, b_out = gate("gate_q5", [[(s, [(t_o1, 0), (s12, 0), (zq, s)])], [(s, [(t_b0, 0), (zq, 0)])]])
    zo, sb = send(o_out, back), send(b_out, swap)
    loss, image_grad, text_grad = call(
        last_kernel,
        "last",
        [jax.ShapeDtypeStruct((1,), F32)] + [shape(s, width)] * 2,
        [own, em, ep, e2, t_o0, zo, sb, images, texts],
        out_specs=(SMEM, VMEM, VMEM),
    )
    return (loss, image_grad, text_grad)


def solution(mesh):
    return jax.shard_map(
        per_device,
        mesh=mesh,
        in_specs=(P(("wide", "narrow"), None), P(("narrow", "wide"), None), P(), P()),
        out_specs=(P(), P(("wide", "narrow"), None), P(("narrow", "wide"), None)),
        check_vma=False,
    )
```

```python
import functools

import jax
import jax.numpy as jnp
import numpy as np
from jax import lax
from jax.experimental import pallas as pl
from jax.experimental.pallas import tpu as pltpu
from jax.sharding import PartitionSpec as P

AXES = ("wide", "narrow")
BF = jnp.bfloat16
F32 = jnp.float32
ROWS = 64
BLOCK = 1024
TILE = 256
STEP = 32


def flat(x, y, z, c):
    x, y, z, c = x % 4, y % 4, z % 8, c % 2
    return ((x * 2 + z // 4) * 2 + c) * 16 + y * 4 + z % 4


PLACES = [(x, y, z, c) for x in range(4) for y in range(4) for z in range(8) for c in range(2)]


def table(move):
    return [(flat(*p), flat(*move(*p))) for p in PLACES]


def first_of(k, x, y, z, c):
    return (x + k, y, z, c) if c == 0 else (x, y + k, z, c)


def second_of(k, x, y, z, c):
    return (x, y + k, z, c) if c == 0 else (x + k, y, z, c)


def along_of(k, x, y, z, c):
    return (x, y, z + k, c) if c == 0 else (x, y, z - k, c)


def first(k):
    return table(functools.partial(first_of, k))


def second(k):
    return table(functools.partial(second_of, k))


def along(k):
    return table(functools.partial(along_of, k))


def sibling():
    return table(lambda x, y, z, c: (x, y, z, 1 - c))


def send(value, pairs):
    return lax.ppermute(value, AXES, pairs)


def cat(*parts):
    return jnp.concatenate(parts, axis=0)


LINE = (0, -1, 1, 2)
CHAIN_0 = [(0, 0), (0, 1), (1, 0), (1, 1), (2, 0)]
CHAIN_1 = [(1, 0), (1, 1), (2, 0)]
CHAIN_2 = [(2, 1), (3, 0)]
CHAIN_3 = [(3, 1), (4, 0)]
U = (2.2, 2.2, 8, 8, 1, 8, 4, 4)
GROUPS = (8 * ROWS, 4 * ROWS, 4 * ROWS)


def shard_tables():
    image = np.zeros((256, 17), np.int32)
    text = np.zeros((256, 16), np.int32)
    for place in PLACES:
        me = flat(*place)
        x, y, z, c = place
        image[me] = [flat(*first_of(k, *second_of(j, *place))) for j in LINE for k in LINE] + [x * 4 + y]

        def owner(at, k, sib):
            x, y, z, c = along_of(-k, *at)
            return flat(x, y, z, 1 - c if sib else c)

        twin = (x, y, z, 1 - c)
        held = [owner(place, k, sib) for k, sib in CHAIN_0] + [owner(twin, k, sib) for k, sib in CHAIN_1]
        for chain in (CHAIN_2, CHAIN_3):
            held += [owner(at, k, sib) for at in (place, twin) for k, sib in chain]
        text[me] = [(h % 16) * 16 + h // 16 for h in held]
    return image, text


IMAGE_SHARDS, TEXT_SHARDS = shard_tables()


FLIPS = [(0, 0, 1, 0), (0, 0, 2, 0), (0, 0, 0, 1), (0, 0, 4, 0)]


def flip_of(k, *at):
    return [a ^ b for a, b in zip(at, FLIPS[k])]


def flipped(value, k):
    return send(value, table(functools.partial(flip_of, k)))


def split(value):
    hi = value.astype(BF)
    return hi, (value - hi.astype(F32)).astype(BF)


def dot3(a_hi, a_lo, b_hi, b_lo, dims):
    def one(a, b):
        return lax.dot_general(a, b, (dims, ((), ())), preferred_element_type=F32)

    return one(a_hi, b_hi) + (one(a_hi, b_lo) + one(a_lo, b_hi))


def split_into(hi, lo, parts, spans):
    at = 0
    for p, start, count in spans:

        @pl.loop(0, count // 16)
        def _(i, part=parts[p], start=start, at=at):
            h, l = split(part[pl.ds(pl.multiple_of(start + i * 16, 16), 16), :])
            rows = pl.ds(pl.multiple_of(at + i * 16, 16), 16)
            hi[rows, :] = h
            lo[rows, :] = l

        at += count


def split_kernel(spans, *refs):
    split_into(refs[-2], refs[-1], refs[:-2], spans)


def coefficients(first_shard, rows, shards, params, col_ids, logits, c_hi, c_lo, acc):
    scale, shift = params[0], params[1]
    at = lax.broadcasted_iota(jnp.int32, (STEP, 1), 0)
    for i in range(rows // STEP):
        here = slice(i * STEP, (i + 1) * STEP)
        row_ids = shards[first_shard + i // (ROWS // STEP)] * ROWS + (i % (ROWS // STEP)) * STEP + at
        for c in range(0, logits.shape[1], 128):
            lanes = slice(c, c + 128)
            x = scale * logits[here, lanes] + shift
            same = row_ids == col_ids[:, lanes]
            e = jnp.exp(jnp.where(same, -x, x))
            p = 1.0 + e
            r = pl.reciprocal(p, approx=True)
            r = r * (2.0 - p * r)
            sig = e * r * scale
            h, l = split(jnp.where(same, -sig, sig))
            c_hi[here, lanes] = h
            c_lo[here, lanes] = l
            q = STEP // 4
            ea, eb, ec, ed = (e[j * q : (j + 1) * q, :] for j in range(4))
            u = ea + (eb + ea * eb)
            v = ec + (ed + ec * ed)
            acc = acc + jnp.log1p(u + (v + u * v))
    return acc


def near_kernel(k, spans, shards, params, col_ids, t_hi, t_lo, *refs):
    parts, (c_hi, c_lo, i_hi, i_lo, loss, logits) = refs[:-6], refs[-6:]
    split_into(i_hi, i_lo, parts, spans)
    acc = jnp.zeros((8, 128), F32)
    parts = []
    for c in range(0, logits.shape[1], 256):
        cols = slice(c, c + 256)
        logits[:, cols] = dot3(i_hi[...], i_lo[...], t_hi[cols, :], t_lo[cols, :], ((1,), (1,)))
        parts.append((k * 4, TILE, shards, params, col_ids.at[:, cols], logits.at[:, cols], c_hi.at[:, cols], c_lo.at[:, cols]))
    for part in parts:
        acc = coefficients(*part, acc)
    loss[...] = acc


def group_kernel(count, final, shards, params, col_ids, *refs):
    lines, parts, losses = refs[:8], refs[8:10], refs[10 : 10 + count]
    stores, (t_hi, t_lo, loss, logits) = refs[10 + count : 18 + count], refs[18 + count :]
    split_into(t_hi, t_lo, parts, [(0, 0, parts[0].shape[0]), (1, 0, parts[1].shape[0])])
    acc = jnp.zeros((8, 128), F32)
    for k in range(4):
        rows = slice(k * TILE, (k + 1) * TILE)
        logits[rows, :] = dot3(lines[2 * k][...], lines[2 * k + 1][...], t_hi[...], t_lo[...], ((1,), (1,)))
        if k:
            acc = coefficients(4 * k - 4, TILE, shards, params, col_ids, logits.at[last, :], stores[2 * k - 2], stores[2 * k - 1], acc)
        last = rows
    acc = coefficients(12, TILE, shards, params, col_ids, logits.at[last, :], stores[6], stores[7], acc)
    for part in losses:
        acc = acc + part[...]
    loss[...] = jnp.full(loss.shape, jnp.sum(acc), F32) if final else acc


def fold_kernel(shards, loss, flip, am, bm, ap, bp, down, up, to_m, to_p, mine):
    s = ROWS
    total = (loss[...] + flip[...])[:1, :1]
    row = lax.broadcasted_iota(jnp.int32, mine.shape, 0)
    lane = lax.broadcasted_iota(jnp.int32, mine.shape, 1)
    value = jnp.where((row == 0) & (lane == shards[16]), total, 0.0)
    mine[...] = value
    to_m[:s, :] = am[:s, :] + down[:s, :]
    to_m[s : 2 * s, :] = am[s:, :]
    to_m[2 * s : 3 * s, :] = bm[:s, :] + down[s:, :]
    to_m[3 * s : 4 * s, :] = bm[s:, :]
    to_m[4 * s :, :] = value
    to_p[:s, :] = ap[:s, :]
    to_p[s : 2 * s, :] = ap[s:, :] + up[:s, :]
    to_p[2 * s : 3 * s, :] = bp[:s, :]
    to_p[3 * s : 4 * s, :] = bp[s:, :] + up[s:, :]
    to_p[4 * s :, :] = value


def gate_kernel(count, rule, *refs):
    ins, outs = refs[:count], refs[count:]
    for out, pieces in zip(outs, rule):
        at = 0
        for rows, terms in pieces:
            total = None
            for p, start in terms:
                v = ins[p][start : start + rows, :]
                total = v if total is None else total + v
            out[at : at + rows, :] = total
            at += rows


def store(outs, rule, value):
    for out, spans in zip(outs, rule):
        at = 0
        for start, rows in spans:
            out[at : at + rows, :] = value[start : start + rows, :]
            at += rows


def image_kernel(rule, *refs):
    ins, outs = refs[:12], refs[12:]
    total = None
    for g in range(3):
        d = dot3(*(r[...] for r in ins[4 * g : 4 * g + 4]), ((1,), (0,)))
        total = d if total is None else total + d
    store(outs, rule, total)


def text_kernel(start, stop, rule, *refs):
    ins, outs = refs[:16], refs[16:]
    total = None
    for k in range(4):
        c_hi, c_lo = (r[:, start:stop] for r in ins[2 * k : 2 * k + 2])
        d = dot3(c_hi, c_lo, ins[8 + 2 * k][...], ins[9 + 2 * k][...], ((0,), (0,)))
        total = d if total is None else total + d
    store(outs, rule, total)


VMEM = pl.BlockSpec(memory_space=pltpu.VMEM)
SMEM = pl.BlockSpec(memory_space=pltpu.SMEM)


def unit_kernel(images, texts, iu, tu, x, y, sems):
    copies = [pltpu.make_async_copy(a, b, sems.at[i]) for i, (a, b) in enumerate(((images, x), (texts, y)))]
    for copy in copies:
        copy.start()
    for copy, source, out in zip(copies, (x, y), (iu, tu)):
        copy.wait()
        v = source[...]
        out[...] = v / jnp.sqrt(jnp.sum(v * v, axis=1, keepdims=True) + 1e-06)


def project(parts, source, out):
    d = parts[0]
    for part in parts[1:]:
        d = d + part
    x = source[...]
    norm = jnp.sqrt(jnp.sum(x * x, axis=1, keepdims=True) + 1e-06)
    u = x / norm
    out[...] = (d - u * jnp.sum(d * u, axis=1, keepdims=True)) / norm


def last_kernel(own, em, ep, e2, o0, zo, sb, images, texts, loss, image_grad, text_grad, x, y, sems):
    s = ROWS
    copies = [pltpu.make_async_copy(a, b, sems.at[i]) for i, (a, b) in enumerate(((images, x), (texts, y)))]
    for copy in copies:
        copy.start()
    for copy in copies:
        copy.wait()
    project([own[:s, :], em[:s, :], ep[:s, :], e2[:s, :]], x, image_grad)
    project([o0[...], zo[...], sb[...]], y, text_grad)
    rows = own[s:, :] + em[s:, :] + ep[s:, :] + e2[s:, :]
    loss[0] = jnp.sum(rows) / 16384.0


def shape(rows, cols, dtype=F32):
    return jax.ShapeDtypeStruct((rows, cols), dtype)


class Chain:
    def __init__(self):
        self.token = None

    def call(self, kernel, name, outs, ins, deps=(), scratch=(), vmem=16, special=0, out_specs=None, raw=0, us=0.1):
        outs, ins, deps = tuple(outs), list(ins), list(deps)
        if self.token is not None and not any(self.token is v for v in ins + deps):
            deps.append(self.token)
        count = len(ins)
        anywhere = pl.BlockSpec(memory_space=pl.ANY)

        def body(*refs):
            kernel(*refs[:count], *refs[count + len(deps) :])

        out = pl.pallas_call(
            body,
            out_shape=outs,
            in_specs=[SMEM] * special + [VMEM] * (count - special - raw) + [pl.BlockSpec(memory_space=pltpu.HBM)] * raw + [anywhere] * len(deps),
            out_specs=out_specs or (VMEM,) * len(outs),
            scratch_shapes=scratch,
            compiler_params=pltpu.CompilerParams(vmem_limit_bytes=vmem << 20),
            cost_estimate=pl.CostEstimate(flops=int(us * 1e9), bytes_accessed=1 << 16, transcendentals=0),
            name=name,
        )(*ins, *deps)
        self.token = out[-1]
        return out

    def gate(self, name, rule, deps=()):
        ins = []

        def place(array):
            for i, known in enumerate(ins):
                if known is array:
                    return i
            ins.append(array)
            return len(ins) - 1

        rule = [[(rows, [(place(v), start) for v, start in terms]) for rows, terms in pieces] for pieces in rule]
        outs = [shape(sum(rows for rows, _ in pieces), ins[pieces[0][1][0][0]].shape[1]) for pieces in rule]
        return self.call(functools.partial(gate_kernel, len(ins), rule), name, outs, ins, deps)


def per_device(images, texts, log_scale, bias):
    width = images.shape[1]
    s = ROWS
    me = lax.axis_index("wide") * 16 + lax.axis_index("narrow")
    shards = lax.dynamic_index_in_dim(jnp.asarray(IMAGE_SHARDS), me, 0, keepdims=False)
    text_shards = lax.dynamic_index_in_dim(jnp.asarray(TEXT_SHARDS), me, 0, keepdims=False)
    col_ids = (text_shards[:, None] * ROWS + jnp.arange(ROWS, dtype=jnp.int32)).reshape(1, BLOCK)
    params = jnp.concatenate([jnp.exp(log_scale), bias])
    ids = [col_ids[:, : 8 * s], col_ids[:, 8 * s : 12 * s], col_ids[:, 12 * s :]]
    swap, ahead, back = sibling(), along(1), along(-1)
    up, down = second(1), second(-1)
    chain = Chain()
    call, gate = chain.call, chain.gate

    def copy(rows, *pieces):
        return [(r, [(v, start)]) for r, (v, start) in zip(rows, pieces)]

    buffers = [pltpu.VMEM((s, width), F32)] * 2 + [pltpu.SemaphoreType.DMA((2,))]
    iu, tu = call(unit_kernel, "units", [shape(s, width)] * 2, [images, texts], scratch=buffers, raw=2)
    fm, fp, f2 = send(iu, first(1)), send(iu, first(-1)), send(iu, first(2))
    o1, b0 = send(tu, ahead), send(tu, swap)
    (zb,) = gate("gate_z1", [copy((s, s), (b0, 0), (o1, 0))])
    z2 = send(zb, ahead)
    (l0,) = gate("gate_l", [copy((s, s, s, s), (iu, 0), (fm, 0), (fp, 0), (f2, 0))])
    lm, lp = send(l0, up), send(l0, down)
    zz2, sw1 = gate("gate_z2", [copy((2 * s,), (z2, 0)), copy((s, 2 * s), (o1, 0), (z2, 0))], [shards, params, *ids])
    z3, s1 = send(zz2, ahead), send(sw1, swap)
    near = call(
        functools.partial(split_kernel, [(0, 0, s), (1, 0, s), (2, 0, s), (3, 0, 2 * s), (4, 0, 3 * s)]),
        "split_near",
        [shape(8 * s, width, BF)] * 2,
        [tu, b0, o1, zz2, s1],
    )

    def near_pairs(k, parts, spans):
        return call(
            functools.partial(near_kernel, k, spans),
            f"near{k}",
            [shape(TILE, GROUPS[0], BF)] * 2 + [shape(TILE, width, BF)] * 2 + [shape(8, 128)],
            [shards, params, ids[0], *near, *parts],
            scratch=[pltpu.VMEM((TILE, GROUPS[0]), F32)],
            special=2,
            us=2.5,
        )

    one = [(0, 0, 4 * s)]
    n0 = near_pairs(0, [l0], one)
    (zz3,) = gate("gate_z3", [copy((2 * s,), (z3, 0))])
    z4, s2 = send(zz3, ahead), send(zz3, swap)
    cu, cd = gate("gate_c", [copy((s, s), (lm, 0), (lm, 2 * s)), copy((s, s), (lp, s), (lp, 3 * s))])
    cu, cd = send(cu, up), send(cd, down)
    n1 = near_pairs(1, [lm], one)
    n2 = near_pairs(2, [lp], one)
    (zz4,) = gate("gate_z4", [copy((2 * s,), (z4, 0))])
    s3 = send(zz4, swap)
    n3 = near_pairs(3, [cu, cd], [(0, 0, s), (1, 0, s), (0, s, s), (1, s, s)])
    n = [n0, n1, n2, n3]
    lines = [v for k in range(4) for v in n[k][2:4]]

    def group_pairs(g, name, parts, losses):
        out = call(
            functools.partial(group_kernel, len(losses), g == 2),
            name,
            [shape(TILE, GROUPS[g], BF)] * 8 + [shape(GROUPS[g], width, BF)] * 2 + [shape(8, 128)],
            [shards, params, ids[g], *lines, *parts, *losses],
            scratch=[pltpu.VMEM((BLOCK, GROUPS[g]), F32)],
            special=2,
            us=4.5,
        )
        return out[:8], out[8:10], out[10]

    mid_coeffs, mid, loss = group_pairs(1, "mid", [zz3, s2], [n[k][4] for k in range(4)])
    far_coeffs, far, loss = group_pairs(2, "far", [zz4, s3], [loss])
    near_coeffs = [v for k in range(4) for v in n[k][:2]]

    def text_dirs(name, coeffs, rule, span=None, us=2.2):
        outs = [shape(sum(r for _, r in spans), width) for spans in rule]
        start, stop = span or (0, coeffs[0].shape[1])
        return call(functools.partial(text_kernel, start, stop, rule), name, outs, [*coeffs, *lines], us=us)

    def image_dirs(k, rule, deps=(), us=2.2):
        outs = [shape(sum(r for _, r in spans), width) for spans in rule]
        ins = [*near_coeffs[2 * k : 2 * k + 2], *near, *mid_coeffs[2 * k : 2 * k + 2], *mid]
        ins += [*far_coeffs[2 * k : 2 * k + 2], *far]
        return call(functools.partial(image_kernel, rule), f"image{k}", outs, ins, deps, us=us)

    def add_loss(name, loss, flip):
        return gate(name, [[(8, [(loss, 0), (flip, 0)])]])[0]

    def add_loss(name, loss, flip, deps=()):
        return gate(name, [[(8, [(loss, 0), (flip, 0)])]], deps)[0]

    f = flipped(loss, 0)
    halves = [[(0, 2 * s)], [(2 * s, 2 * s)]]
    c_dn, c_up = image_dirs(3, [[(0, s), (2 * s, s)], [(s, s), (3 * s, s)]], us=U[0])
    c_dn, c_up = send(c_dn, down), send(c_up, up)
    p34, sw = text_dirs("text_far", far_coeffs, halves, us=U[1])
    s34 = send(sw, swap)
    loss = add_loss("loss1", loss, f)
    f = flipped(loss, 1)
    im1, ib1 = image_dirs(1, halves, us=U[2])
    loss = add_loss("loss2", loss, f)
    f = flipped(loss, 2)
    im2, ib2 = image_dirs(2, halves, us=U[3])
    loss = add_loss("loss3", loss, f)
    f = flipped(loss, 3)
    (z_out,) = gate("gate_q1", [[(2 * s, [(p34, 0), (s34, 0)])]])
    zq = send(z_out, back)
    p23, sw = text_dirs("text_mid", mid_coeffs, halves, us=U[4])
    s23 = send(sw, swap)
    t_12, sw = text_dirs("text_near", near_coeffs, [[(0, 2 * s)], [(2 * s, 3 * s)]], (3 * s, 8 * s), us=U[5])
    s12 = send(sw, swap)
    to_m, to_p, mine = call(
        fold_kernel,
        "fold",
        [shape(4 * s + 8, width)] * 2 + [shape(8, width)],
        [shards, loss, f, im1, ib1, im2, ib2, c_dn, c_up],
        special=1,
    )
    lm, lp, across = send(to_m, down), send(to_p, up), send(mine, second(2))
    (z_out,) = gate("gate_q2", [[(2 * s, [(p23, 0), (s23, 0), (zq, 0)])]])
    zq = send(z_out, back)
    t_o0, t_b0, t_o1 = text_dirs("text_own", near_coeffs, [[(0, s)], [(s, s)], [(2 * s, s)]], (0, 3 * s), us=U[6])
    im0, ib0 = image_dirs(0, halves, us=U[7])
    (z_out,) = gate("gate_q3", [[(2 * s, [(t_12, 0), (s12, s), (zq, 0)])]])
    zq = send(z_out, back)
    rows = (8, [(mine, 0), (lm, 4 * s), (lp, 4 * s), (across, 0)])
    own, e_fm, e_fp, e_f2 = gate(
        "gate_q4",
        [
            [(s, [(im0, 0), (lm, 0), (lp, 0)]), rows],
            [(s, [(im0, s), (lm, s), (lp, s)]), rows],
            [(s, [(ib0, 0), (lm, 2 * s), (lp, 2 * s)]), rows],
            [(s, [(ib0, s), (lm, 3 * s), (lp, 3 * s)]), rows],
        ],
    )
    em, ep, e2 = send(e_fm, first(-1)), send(e_fp, first(1)), send(e_f2, first(2))
    o_out, b_out = gate("gate_q5", [[(s, [(t_o1, 0), (s12, 0), (zq, s)])], [(s, [(t_b0, 0), (zq, 0)])]])
    zo, sb = send(o_out, back), send(b_out, swap)
    loss, image_grad, text_grad = call(
        last_kernel,
        "last",
        [jax.ShapeDtypeStruct((1,), F32)] + [shape(s, width)] * 2,
        [own, em, ep, e2, t_o0, zo, sb, images, texts],
        scratch=buffers,
        out_specs=(SMEM, VMEM, VMEM),
        raw=2,
    )
    return (loss, image_grad, text_grad)


def solution(mesh):
    return jax.shard_map(
        per_device,
        mesh=mesh,
        in_specs=(P(("wide", "narrow"), None), P(("narrow", "wide"), None), P(), P()),
        out_specs=(P(), P(("wide", "narrow"), None), P(("narrow", "wide"), None)),
        check_vma=False,
    )
```
